32 devices in a mesh: outer: 4 (over y, x), inner: 8 (over z, core).
Axes of the slice: x: 2, y: 2, z: 4, core: 2. Of those that a mesh axis runs over, the one named last changes fastest.
Arguments:
- vectors: bfloat16 [65536, 256], P(('outer', 'inner')), may hold values from -6 to 6
- leaf_basis: bfloat16 [65536, 256], P(('outer', 'inner')), may hold values from -0.375 to 0.375
- transfer: bfloat16 [4, 4, 8, 8, 512, 256], P(None, 'outer', 'inner'), may hold values from -0.25 to 0.25
- core_mats: bfloat16 [4, 8, 8, 256, 256], P('outer', 'inner'), may hold values from -0.375 to 0.375
- row_basis: bfloat16 [65536, 256], P(('outer', 'inner')), may hold values from -0.375 to 0.375
- box_order: int32 [4, 8, 8], P('outer', 'inner'), may hold values from 0 to 7, each once within a row
Outputs:
- applied: bfloat16 [65536, 256], P(('outer', 'inner'))
The draws below stay inside these ranges and needn't reach their ends.
Inputs may be any that keep to these rules, and one draw needn't show every extreme that they name: `box_order`: for every device the 8 entries are a permutation of 0 to 7.
All inputs are finite; a program needn't handle non-finite values.
Results may differ from the reference program's by a relative error of at most 0.011.
Values may be sent and summed in bfloat16 or wider, within the bound.
No kernel may reach another device: no remote copies, remote signals or barrier semaphores. Data moves between devices by JAX's collectives and lax.ppermute only.
A program may use at most 64 MiB of HBM per device.

```python
import jax
import jax.numpy as jnp
from jax import lax

R = 256
BOX_DEV = 8
LEVELS = 4
LEAF = 256
C = 256
ROWS = 65536
N_OUTER = 4
N_INNER = 8


def level_of(own_key, extent, cuts, low, top_value):
    def one(dim, parts):
        heights = jax.random.uniform(jax.random.fold_in(jax.random.fold_in(own_key, 6), dim), (parts,), jnp.float32, low / len(cuts), top_value / len(cuts))
        return jnp.repeat(jnp.exp(heights), extent[dim] // parts).reshape((-1,) + (1,) * (len(extent) - dim - 1))

    factor_of = one(*cuts[0])
    for cut in cuts[1:]:
        factor_of = factor_of * one(*cut)
    return factor_of


def noise(rng, dims, deviation, reach, cuts=(), kind=jnp.bfloat16):
    entries = deviation * jax.random.normal(rng, dims, jnp.float32)
    if cuts:
        entries = entries * level_of(rng, dims, cuts, -0.22, 0.18)
    return jnp.clip(entries, -reach, reach).astype(kind)


def setup_inputs(seed: int = 0) -> dict:
    splits = jax.random.split(jax.random.key(seed), 7)
    return {
        "vectors": noise(splits[0], (ROWS, C), 1.0, 6.0, ((0, 32),)),
        "leaf_basis": noise(splits[1], (ROWS, R), LEAF ** -0.5, 0.375, ((0, 32),)),
        "transfer": noise(splits[2], (LEVELS, N_OUTER, N_INNER, BOX_DEV, 2 * R, R), (2 * R) ** -0.5, 0.25, ((1, 4), (2, 8))),
        "core_mats": noise(splits[3], (N_OUTER, N_INNER, BOX_DEV, R, R), R ** -0.5, 0.375, ((0, 4), (1, 8))),
        "row_basis": noise(splits[4], (ROWS, R), R ** -0.5, 0.375, ((0, 32),)),
        "box_order": jax.vmap(lambda own: jax.random.permutation(own, BOX_DEV))(jax.random.split(splits[5], N_OUTER * N_INNER)).reshape((N_OUTER, N_INNER, BOX_DEV)).astype(jnp.int32),
    }


def widen(values):
    return lax.optimization_barrier(values).astype(jnp.float32)


def reference(vectors, leaf_basis, transfer, core_mats, row_basis, box_order):
    dev_count = N_OUTER * N_INNER
    half_count = BOX_DEV // 2
    x_boxes = vectors.reshape(dev_count, BOX_DEV, LEAF, C).astype(jnp.float32)
    v_boxes = leaf_basis.reshape(dev_count, BOX_DEV, LEAF, R).astype(jnp.float32)
    box_state = jnp.einsum('dklc,dklr->dkcr', x_boxes, v_boxes).astype(jnp.bfloat16)
    weights = transfer.reshape(LEVELS, dev_count, half_count, 2, 2 * R, R)
    device_ids = jnp.arange(dev_count, dtype=jnp.int32)
    inner_bits = N_INNER.bit_length() - 1
    bit_list = [0, 1, inner_bits, inner_bits + 1]
    for level_idx in range(LEVELS):
        bit_pos = bit_list[level_idx]
        partner = jnp.bitwise_xor(device_ids, jnp.int32(1 << bit_pos))
        half_flag = jnp.bitwise_and(jnp.right_shift(device_ids, jnp.int32(bit_pos)), jnp.int32(1))
        low_dev = jnp.where(half_flag == 0, device_ids, partner)
        high_dev = jnp.where(half_flag == 0, partner, device_ids)
        halves = box_state.reshape(dev_count, 2, half_count, C, R)
        low_half = halves[low_dev, half_flag]
        high_half = halves[high_dev, half_flag]
        stacked = widen(jnp.concatenate([low_half, high_half], axis=3))
        level_w = weights[level_idx].astype(jnp.float32)
        merged = jnp.einsum('dkcs,dkosr->dkocr', stacked, level_w)
        box_state = merged.reshape(dev_count, BOX_DEV, C, R).astype(jnp.bfloat16)
    slot_order = box_order.reshape(dev_count, BOX_DEV)
    chosen = widen(jnp.take_along_axis(box_state, slot_order[:, :, None, None], axis=1))
    cores = core_mats.reshape(dev_count, BOX_DEV, R, R).astype(jnp.float32)
    core_out = jnp.einsum('dkcs,dksr->dkcr', chosen, cores).astype(jnp.bfloat16)
    u_boxes = row_basis.reshape(dev_count, BOX_DEV, LEAF, R).astype(jnp.float32)
    boxed = jnp.einsum('dklr,dkcr->dklc', u_boxes, widen(core_out)).astype(jnp.bfloat16)
    piece_rows = BOX_DEV * LEAF // N_INNER
    placed = boxed.reshape(N_OUTER, N_INNER, N_INNER, piece_rows, C).transpose(0, 2, 1, 3, 4)
    return placed.reshape(ROWS, C)
```

```python
import functools

import jax
import jax.numpy as jnp
from jax import lax
from jax.experimental import pallas as pl
from jax.experimental.pallas import tpu as pltpu
from jax.sharding import PartitionSpec as P

INNER_LEVELS = 2
PARTS = (4, 5, 7)
VMEM = pl.BlockSpec(memory_space=pltpu.VMEM)
ANY = pl.BlockSpec(memory_space=pl.ANY)
SMEM = pl.BlockSpec(memory_space=pltpu.SMEM)


def swapped(array, axis, step):
    return lax.ppermute(array, axis, [(i, i ^ step) for i in range(lax.axis_size(axis))])


def level_axis(level):
    return ("inner", level) if level < INNER_LEVELS else ("outer", level - INNER_LEVELS)


def bit_of(level):
    axis, bit = level_axis(level)
    return jnp.bitwise_and(jnp.right_shift(lax.axis_index(axis), bit), 1)


def dot(a, b, dims):
    return lax.dot_general(a, b, (dims, ((), ())), preferred_element_type=jnp.float32).astype(
        jnp.bfloat16
    )


def call(kernel, outs, ins, specs, flops, scratch=()):
    moved = sum(x.size * x.dtype.itemsize for x in list(ins) + list(outs))
    return pl.pallas_call(
        kernel,
        out_shape=outs,
        in_specs=specs,
        out_specs=[VMEM] * len(outs),
        scratch_shapes=list(scratch),
        compiler_params=pltpu.CompilerParams(vmem_limit_bytes=32 * 1024 * 1024),
        cost_estimate=pl.CostEstimate(flops=flops, bytes_accessed=moved, transcendentals=0),
    )(*ins)


def leaf_kernel(cuts, x_ref, v_ref, *outs):
    half = outs[0].shape[0]
    flag = bit_of(0)
    rows = x_ref.shape[0] // (2 * half)
    for slot in range(2 * half):
        side = 1 - flag if slot < half else flag
        box = side * half + slot % half
        window = pl.ds(pl.multiple_of(box * rows, rows), rows)
        state = dot(x_ref[window, :].T, v_ref[window, :], ((1,), (0,)))
        for n, (begin, size) in enumerate(cuts):
            outs[2 * n + (slot >= half)][slot % half] = state[begin : begin + size]


def merge_box(level, kept_ref, got_ref, w_ref, begin, size, k, o):
    rank = kept_ref.shape[2]
    flag = bit_of(level)
    mine = w_ref[level, 0, 0, 2 * k + o, pl.ds(pl.multiple_of(flag * rank, rank), rank), :]
    other = w_ref[level, 0, 0, 2 * k + o, pl.ds(pl.multiple_of((1 - flag) * rank, rank), rank), :]
    dims = (((1,), (0,)), ((), ()))
    total = lax.dot_general(
        kept_ref[k, begin : begin + size], mine, dims, preferred_element_type=jnp.float32
    )
    total += lax.dot_general(
        got_ref[k, begin : begin + size], other, dims, preferred_element_type=jnp.float32
    )
    return total.astype(jnp.bfloat16)


def merge_kernel(level, begin, size, kept_ref, got_ref, w_ref, after_ref, sent_out, kept_out):
    half = kept_ref.shape[0]
    flag = bit_of(level + 1)
    for slot in range(2 * half):
        side = 1 - flag if slot < half else flag
        box = side * half + slot % half
        out = sent_out if slot < half else kept_out
        k = box // 2
        out[slot % half] = merge_box(level, kept_ref, got_ref, w_ref, begin, size, k, slot % 2)


def last_kernel(
    level, begin, size, order_ref, kept_ref, got_ref, w_ref, core_ref, u_ref, after_ref,
    cross_out, mine_out, state, cored,
):
    half = kept_ref.shape[0]
    pieces = 2 * cross_out.shape[0]
    leaf_rows = u_ref.shape[0] // (2 * half)
    rows = u_ref.shape[0] // pieces
    me = lax.axis_index("inner")
    for box in range(2 * half):
        state[box] = merge_box(level, kept_ref, got_ref, w_ref, begin, size, box // 2, box % 2)
    for box in range(2 * half):
        cored[box] = dot(state[order_ref[0, 0, box]], core_ref[0, 0, box], ((1,), (0,)))
    width = min(rows, leaf_rows)
    for t in range(pieces // 2):
        for out, step in ((cross_out, 2 * t + 1), (mine_out, 2 * t)):
            first = jnp.bitwise_xor(me, step) * rows
            for at in range(0, rows, width):
                row = pl.multiple_of(first + at, width)
                out[t, :, at : at + width] = dot(
                    cored[row // leaf_rows], u_ref[pl.ds(row, width), :], ((1,), (1,))
                )


def pack_kernel(got_ref, mine_ref, *outs):
    for t, out in enumerate(outs, 1):
        out[0] = mine_ref[t]
        out[1] = got_ref[t]


def place_kernel(cuts, *refs):
    out, ins = refs[-1], refs[:-1]
    me = lax.axis_index("inner")
    per = len(ins) // len(cuts)
    for n, (begin, size) in enumerate(cuts):
        got_ref, mine_ref, *others = ins[n * per : (n + 1) * per]
        rows = mine_ref.shape[2]
        for t in range(per - 1):
            for odd in range(2):
                if t == 0:
                    block = (got_ref if odd else mine_ref)[0]
                else:
                    block = others[t - 1][odd]
                owner = jnp.bitwise_xor(me, 2 * t + odd)
                window = pl.ds(pl.multiple_of(owner * rows, rows), rows)
                out[window, begin : begin + size] = block.T


def on_device(vectors, leaf_basis, transfer, core_mats, row_basis, box_order):
    boxes = transfer.shape[3]
    half = boxes // 2
    rank = leaf_basis.shape[1]
    columns = vectors.shape[1]
    levels = transfer.shape[0]
    inner = lax.axis_size("inner")
    piece = vectors.shape[0] // inner
    edges = [columns * sum(PARTS[:n]) // sum(PARTS) for n in range(len(PARTS) + 1)]
    cuts = [(a, b - a) for a, b in zip(edges, edges[1:])]

    def arr(*shape):
        return jax.ShapeDtypeStruct(shape, jnp.bfloat16)

    firsts = [cuts[0], (cuts[1][0], columns - cuts[1][0])]
    outs = call(
        functools.partial(leaf_kernel, firsts),
        [arr(half, size, rank) for _, size in firsts for _ in range(2)],
        [vectors, leaf_basis],
        [VMEM, VMEM],
        2 * columns * rank * vectors.shape[0],
    )
    sent_a, kept_a, sent_b, kept_b = outs
    got_a, got_b = swapped(sent_a, "inner", 1), swapped(sent_b, "inner", 1)
    held = [(kept_a, got_a, 0)]
    held += [(kept_b, got_b, begin - cuts[1][0]) for begin, _ in cuts[1:]]

    after = kept_b
    done = [None] * len(cuts)
    steps = sorted((n + 2 * l, -n, n, l) for n in range(len(cuts)) for l in range(levels))
    for _, _, n, level in steps:
        size = cuts[n][1]
        kept, got, begin = held[n]
        flops = 2 * boxes * size * 2 * rank * rank
        if level < levels - 1:
            sent, kept = call(
                functools.partial(merge_kernel, level, begin, size),
                [arr(half, size, rank)] * 2,
                [kept, got, transfer, after],
                [VMEM, VMEM, VMEM, ANY],
                flops,
            )
            after = kept
            axis, bit = level_axis(level + 1)
            held[n] = (kept, swapped(sent, axis, 1 << bit), 0)
        else:
            cross, mine = call(
                functools.partial(last_kernel, level, begin, size),
                [arr(inner // 2, size, piece)] * 2,
                [box_order, kept, got, transfer, core_mats, row_basis, after],
                [SMEM, VMEM, VMEM, VMEM, VMEM, VMEM, ANY],
                2 * flops,
                [pltpu.VMEM((boxes, size, rank), jnp.bfloat16)] * 2,
            )
            after = mine
            got = swapped(cross, "inner", 1)
            packed = call(
                pack_kernel,
                [arr(2, size, piece)] * (inner // 2 - 1),
                [got, mine],
                [VMEM, VMEM],
                0,
            )
            others = [swapped(p, "inner", 2 * t) for t, p in enumerate(packed, 1)]
            done[n] = [got, mine, *others]
    flat = [x for part in done for x in part]
    return call(
        functools.partial(place_kernel, cuts), [arr(*vectors.shape)], flat, [VMEM] * len(flat), 0
    )[0]


def solution(mesh):
    in_specs = (
        P(("outer", "inner"), None),
        P(("outer", "inner"), None),
        P(None, "outer", "inner", None, None, None),
        P("outer", "inner", None, None, None),
        P(("outer", "inner"), None),
        P("outer", "inner", None),
    )
    out_specs = P(("outer", "inner"), None)
    return jax.shard_map(
        on_device, mesh=mesh, in_specs=in_specs, out_specs=out_specs, check_vma=False
    )
```

```python
import functools

import jax
import jax.numpy as jnp
from jax import lax
from jax.experimental import pallas as pl
from jax.experimental.pallas import tpu as pltpu
from jax.sharding import PartitionSpec as P

INNER_LEVELS = 2
PARTS = (4, 5, 7)
COSTS = {}
ORDER = ("f", "w", "m0a", "m0b", "m0c", "m1a", "m1b", "j", "m2a", "m1c", "m2b", "oa", "m2c", "ob", "qa", "ec", "pc", "qb")
LEAF_ROOM = 52
LOAD_ROOM = 48
HBM = pl.BlockSpec(memory_space=pltpu.HBM)
VMEM = pl.BlockSpec(memory_space=pltpu.VMEM)
ANY = pl.BlockSpec(memory_space=pl.ANY)
SMEM = pl.BlockSpec(memory_space=pltpu.SMEM)


def swapped(array, axis, step):
    return lax.ppermute(array, axis, [(i, i ^ step) for i in range(lax.axis_size(axis))])


def level_axis(level):
    return ("inner", level) if level < INNER_LEVELS else ("outer", level - INNER_LEVELS)


def bit_of(level):
    axis, bit = level_axis(level)
    return jnp.bitwise_and(jnp.right_shift(lax.axis_index(axis), bit), 1)


def arr(*shape):
    return jax.ShapeDtypeStruct(shape, jnp.bfloat16)


def dot(a, b, dims=((1,), (0,))):
    return lax.dot_general(a, b, (dims, ((), ())), preferred_element_type=jnp.float32)


def call(kernel, outs, ins, specs, scratch=(), name=None, room=24):
    run = pl.pallas_call(
        kernel,
        name=name,
        out_shape=outs,
        in_specs=specs,
        out_specs=[VMEM] * len(outs),
        scratch_shapes=list(scratch),
        compiler_params=pltpu.CompilerParams(vmem_limit_bytes=room * 1024 * 1024),
        cost_estimate=pl.CostEstimate(
            flops=int(COSTS.get(name, 2) * 1e9), bytes_accessed=0, transcendentals=0
        ),
    )
    return list(run(*ins))


def copy_all(copies):
    for copy in copies:
        copy.start()
    return copies


def load_kernel(w_hbm, after_ref, w_out, sem):
    load = pltpu.make_async_copy(w_hbm.at[0, 0, 0], w_out, sem)
    load.start()
    load.wait()


def leaf_kernel(cuts, x_hbm, v_hbm, *refs):
    outs, (x_ref, v_ref, sems) = refs[:-3], refs[-3:]
    half = outs[0].shape[0]
    flag = bit_of(0)
    rows = x_ref.shape[0] // (2 * half)

    def window(slot):
        side = 1 - flag if slot < half else flag
        return pl.ds(pl.multiple_of((side * half + slot % half) * rows, rows), rows)

    loads = []
    for slot in range(2 * half):
        at = window(slot)
        loads.append(
            copy_all(
                [
                    pltpu.make_async_copy(x_hbm.at[at], x_ref.at[at], sems.at[0, slot]),
                    pltpu.make_async_copy(v_hbm.at[at], v_ref.at[at], sems.at[1, slot]),
                ]
            )
        )
    for slot in range(2 * half):
        at = window(slot)
        for load in loads[slot]:
            load.wait()
        state = dot(x_ref[at, :].T, v_ref[at, :]).astype(jnp.bfloat16)
        for n, (begin, size) in enumerate(cuts):
            outs[2 * n + (slot >= half)][slot % half] = state[begin : begin + size]


def join_kernel(level, order_ref, w_ref, core_ref, u_ref, after_ref, joint_out):
    width = joint_out.shape[2]
    for n in range(joint_out.shape[0]):
        box = n * width // (u_ref.shape[0] // core_ref.shape[2])
        inside = dot(core_ref[0, 0, box], u_ref[n * width : (n + 1) * width, :], ((1,), (1,)))
        joint = dot(w_ref[level, 0, 0, order_ref[0, 0, box]], inside.astype(jnp.bfloat16))
        joint_out[n] = joint.astype(jnp.bfloat16)


def merged(level, begin, size, kept_ref, got_ref, w_ref, k, box):
    rank = kept_ref.shape[2]
    flag = bit_of(level)
    at = pl.ds(begin, size)
    place = (level, 0, 0, box) if len(w_ref.shape) == 6 else (box,)
    mine = w_ref[(*place, pl.ds(pl.multiple_of(flag * rank, rank), rank), slice(None))]
    other = w_ref[(*place, pl.ds(pl.multiple_of((1 - flag) * rank, rank), rank), slice(None))]
    total = dot(kept_ref[k, at, :], mine) + dot(got_ref[k, at, :], other)
    return total.astype(jnp.bfloat16)


def merge_kernel(level, begin, size, kept_ref, got_ref, w_ref, after_ref, sent_out, kept_out):
    half = kept_ref.shape[0]
    flag = bit_of(level + 1)
    for slot in range(2 * half):
        side = 1 - flag if slot < half else flag
        box = side * half + slot % half
        out = sent_out if slot < half else kept_out
        out[slot % half] = merged(level, begin, size, kept_ref, got_ref, w_ref, box // 2, box)


def last_kernel(
    level, early, begin, size, order_ref, kept_ref, got_ref, joint_ref, after_ref, *outs
):
    half = kept_ref.shape[0]
    me = lax.axis_index("inner")
    width = joint_ref.shape[2]
    piece = outs[0].shape[2]
    pieces = joint_ref.shape[0] * width // piece
    per_box = joint_ref.shape[0] // (2 * half)
    for t in range(pieces // 2):
        for odd in range(2):
            out = (outs[1 + t] if odd else outs[0].at[t]) if early else outs[t].at[odd]
            first = jnp.bitwise_xor(me, 2 * t + odd) * (piece // width)
            for n in range(piece // width):
                k = order_ref[0, 0, (first + n) // per_box] // 2
                out[:, n * width : (n + 1) * width] = merged(
                    level, begin, size, kept_ref, got_ref, joint_ref, k, first + n
                )


def early_pack_kernel(mine_ref, *refs):
    count = mine_ref.shape[0]
    for t, out in enumerate(refs[count + 1 :], 1):
        out[0] = mine_ref[t]
        out[1] = refs[t][...]


def late_pack_kernel(*refs):
    out = refs[-1]
    for t, ref in enumerate(refs[:-2]):
        out[t] = ref[1]


def place_kernel(cuts, *refs):
    out, ins = refs[-1], refs[:-1]
    me = lax.axis_index("inner")
    rows = ins[0].shape[2]
    per = out.shape[0] // rows // 2 + 1
    for n, (begin, size) in enumerate(cuts):
        chunk = ins[n * per : (n + 1) * per]
        last = n == len(cuts) - 1
        for t in range(per - 1):
            for odd in range(2):
                if last:
                    block = chunk[t + 1][odd]
                    if t == 0:
                        block = chunk[1][...] if odd else chunk[0][0]
                else:
                    block = chunk[per - 1][t] if odd else chunk[t][0]
                owner = jnp.bitwise_xor(me, 2 * t + odd)
                window = pl.ds(pl.multiple_of(owner * rows, rows), rows)
                out[window, begin : begin + size] = block.T


def on_device(vectors, leaf_basis, transfer, core_mats, row_basis, box_order):
    boxes = transfer.shape[3]
    half = boxes // 2
    rank = leaf_basis.shape[1]
    columns = vectors.shape[1]
    levels = transfer.shape[0]
    inner = lax.axis_size("inner")
    piece = vectors.shape[0] // inner
    width = min(piece, vectors.shape[0] // boxes)
    edges = [columns * sum(PARTS[:n]) // sum(PARTS) for n in range(len(PARTS) + 1)]
    cuts = [(a, b - a) for a, b in zip(edges, edges[1:])]
    count = len(cuts)
    held = [None] * count
    done = [None] * count
    level_w = joint = after = None

    for step in ORDER:
        kind, n = step[0], "abcdefgh".find(step[-1])
        if kind == "f":
            firsts = [cuts[0], (cuts[1][0], columns - cuts[1][0])]
            sent_a, kept_a, sent_b, kept_b = call(
                functools.partial(leaf_kernel, firsts),
                [arr(half, size, rank) for _, size in firsts for _ in range(2)],
                [vectors, leaf_basis],
                [HBM] * 2,
                [
                    pltpu.VMEM(vectors.shape, jnp.bfloat16),
                    pltpu.VMEM(leaf_basis.shape, jnp.bfloat16),
                    pltpu.SemaphoreType.DMA((2, boxes)),
                ],
                name="leaves",
                room=LEAF_ROOM,
            )
            got_a, got_b = swapped(sent_a, "inner", 1), swapped(sent_b, "inner", 1)
            held = [(kept_a, got_a, 0)]
            held += [(kept_b, got_b, begin - cuts[1][0]) for begin, _ in cuts[1:]]
            after = kept_b
        elif kind == "w":
            level_w = call(
                load_kernel,
                [arr(boxes, 2 * rank, rank)],
                [transfer, after],
                [HBM, ANY],
                [pltpu.SemaphoreType.DMA],
                name="weights",
                room=LOAD_ROOM,
            )[0]
            after = level_w
        elif kind == "j":
            joint = call(
                functools.partial(join_kernel, levels - 1),
                [arr(vectors.shape[0] // width, 2 * rank, width)],
                [box_order, transfer, core_mats, row_basis, after],
                [SMEM, VMEM, VMEM, VMEM, ANY],
                name="join",
            )[0]
            after = joint
        elif kind == "m":
            level = int(step[1])
            size = cuts[n][1]
            kept, got, begin = held[n]
            sent, kept = call(
                functools.partial(merge_kernel, level, begin, size),
                [arr(half, size, rank)] * 2,
                [kept, got, transfer if level else level_w, after],
                [VMEM, VMEM, VMEM, ANY],
                name=f"merge{level}{step[-1]}",
            )
            after = kept
            axis, bit = level_axis(level + 1)
            held[n] = (kept, swapped(sent, axis, 1 << bit), 0)
        elif kind in "eo":
            size = cuts[n][1]
            kept, got, begin = held[n]
            early = kind == "e"
            shapes = [arr(2, size, piece)] * (inner // 2)
            if early:
                shapes = [arr(inner // 2, size, piece)] + [arr(size, piece)] * (inner // 2)
            outs = call(
                functools.partial(last_kernel, levels - 1, early, begin, size),
                shapes,
                [box_order, kept, got, joint, after],
                [SMEM, VMEM, VMEM, VMEM, ANY],
                name=f"last{step[-1]}",
            )
            after = outs[0]
            if early:
                done[n] = outs[:1] + [swapped(x, "inner", 1) for x in outs[1:]]
            else:
                done[n] = outs[:1] + [swapped(x, "inner", 2 * t) for t, x in enumerate(outs[1:], 1)]
        elif kind == "p":
            outs = call(
                early_pack_kernel,
                [arr(2, cuts[n][1], piece)] * (inner // 2 - 1),
                done[n] + [after],
                [VMEM] * len(done[n]) + [ANY],
                name=f"pack{step[-1]}",
            )
            after = outs[0]
            done[n] = done[n][:2] + [swapped(x, "inner", 2 * t) for t, x in enumerate(outs, 1)]
        elif kind == "q":
            cross = call(
                late_pack_kernel,
                [arr(inner // 2, cuts[n][1], piece)],
                done[n] + [after],
                [VMEM] * len(done[n]) + [ANY],
                name=f"pack{step[-1]}",
            )[0]
            after = cross
            done[n].append(swapped(cross, "inner", 1))
    flat = [x for part in done for x in part]
    return call(
        functools.partial(place_kernel, cuts),
        [arr(*vectors.shape)],
        flat,
        [VMEM] * len(flat),
        name="place",
    )[0]


def solution(mesh):
    in_specs = (
        P(("outer", "inner"), None),
        P(("outer", "inner"), None),
        P(None, "outer", "inner", None, None, None),
        P("outer", "inner", None, None, None),
        P(("outer", "inner"), None),
        P("outer", "inner", None),
    )
    out_specs = P(("outer", "inner"), None)
    return jax.shard_map(
        on_device, mesh=mesh, in_specs=in_specs, out_specs=out_specs, check_vma=False
    )
```

```python
import functools

import jax
import jax.numpy as jnp
from jax import lax
from jax.experimental import pallas as pl
from jax.experimental.pallas import tpu as pltpu
from jax.sharding import PartitionSpec as P

INNER_LEVELS = 2
PARTS = (4, 5, 7)
COSTS = {"merge2c":.4,"lastb":.1,"lastc":.4,"packc":0,"lasta":1,"packa":2,"packb":1,"merge1b":.4,"join":.3,"inside":.3,"merge2a":.4,"merge1a":1}
ORDER = ("f", "w", "m0a", "m0b", "m0c", "i", "m1a", "m1b", "j", "m2a", "m1c", "m2b", "oa", "m2c", "ob", "qa", "oc", "qb", "rc")
LEAF_ROOM = 52
LOAD_ROOM = 48
HBM = pl.BlockSpec(memory_space=pltpu.HBM)
VMEM = pl.BlockSpec(memory_space=pltpu.VMEM)
ANY = pl.BlockSpec(memory_space=pl.ANY)
SMEM = pl.BlockSpec(memory_space=pltpu.SMEM)


def turns(count):
    return sorted(range(1, count), key=lambda t: (t < count // 2, t))


def swapped(array, axis, step):
    return lax.ppermute(array, axis, [(i, i ^ step) for i in range(lax.axis_size(axis))])


def level_axis(level):
    return ("inner", level) if level < INNER_LEVELS else ("outer", level - INNER_LEVELS)


def bit_of(level):
    axis, bit = level_axis(level)
    return jnp.bitwise_and(jnp.right_shift(lax.axis_index(axis), bit), 1)


def arr(*shape):
    return jax.ShapeDtypeStruct(shape, jnp.bfloat16)


def dot(a, b, dims=((1,), (0,))):
    return lax.dot_general(a, b, (dims, ((), ())), preferred_element_type=jnp.float32)


def call(kernel, outs, ins, specs, scratch=(), name=None, room=24, out_spec=VMEM):
    run = pl.pallas_call(
        kernel,
        name=name,
        out_shape=outs,
        in_specs=specs,
        out_specs=[out_spec] * len(outs),
        scratch_shapes=list(scratch),
        compiler_params=pltpu.CompilerParams(vmem_limit_bytes=room * 1024 * 1024),
        cost_estimate=pl.CostEstimate(
            flops=int(COSTS.get(name, 2) * 1e9), bytes_accessed=0, transcendentals=0
        ),
    )
    return list(run(*ins))


def copy_all(copies):
    for copy in copies:
        copy.start()
    return copies


def load_kernel(w_hbm, after_ref, w_out, sem):
    load = pltpu.make_async_copy(w_hbm.at[0, 0, 0], w_out, sem)
    load.start()
    load.wait()


def leaf_kernel(cuts, x_hbm, v_hbm, *refs):
    outs, (x_ref, v_ref, sems) = refs[:-3], refs[-3:]
    half = outs[0].shape[0]
    flag = bit_of(0)
    rows = x_ref.shape[0] // (2 * half)

    def window(slot):
        side = 1 - flag if slot < half else flag
        return pl.ds(pl.multiple_of((side * half + slot % half) * rows, rows), rows)

    loads = []
    for slot in range(2 * half):
        at = window(slot)
        loads.append(
            copy_all(
                [
                    pltpu.make_async_copy(x_hbm.at[at], x_ref.at[at], sems.at[0, slot]),
                    pltpu.make_async_copy(v_hbm.at[at], v_ref.at[at], sems.at[1, slot]),
                ]
            )
        )
    for slot in range(2 * half):
        at = window(slot)
        for load in loads[slot]:
            load.wait()
        state = dot(x_ref[at, :].T, v_ref[at, :]).astype(jnp.bfloat16)
        for n, (begin, size) in enumerate(cuts):
            outs[2 * n + (slot >= half)][slot % half] = state[begin : begin + size]


def inside_kernel(core_ref, u_ref, after_ref, out):
    width = out.shape[2]
    for n in range(out.shape[0]):
        box = n * width // (u_ref.shape[0] // core_ref.shape[2])
        inside = dot(core_ref[0, 0, box], u_ref[n * width : (n + 1) * width, :], ((1,), (1,)))
        out[n] = inside.astype(jnp.bfloat16)


def join_kernel(level, order_ref, w_ref, inside_ref, after_ref, out):
    per_box = inside_ref.shape[0] // w_ref.shape[3]
    for n in range(out.shape[0]):
        joint = dot(w_ref[level, 0, 0, order_ref[0, 0, n // per_box]], inside_ref[n])
        out[n] = joint.astype(jnp.bfloat16)


def merged(level, begin, size, kept_ref, got_ref, w_ref, k, box):
    rank = kept_ref.shape[2]
    flag = bit_of(level)
    at = pl.ds(begin, size)
    place = (level, 0, 0, box) if len(w_ref.shape) == 6 else (box,)
    mine = w_ref[(*place, pl.ds(pl.multiple_of(flag * rank, rank), rank), slice(None))]
    other = w_ref[(*place, pl.ds(pl.multiple_of((1 - flag) * rank, rank), rank), slice(None))]
    total = dot(kept_ref[k, at, :], mine) + dot(got_ref[k, at, :], other)
    return total.astype(jnp.bfloat16)


def merge_kernel(level, begin, size, kept_ref, got_ref, w_ref, after_ref, sent_out, kept_out):
    half = kept_ref.shape[0]
    flag = bit_of(level + 1)
    for slot in range(2 * half):
        side = 1 - flag if slot < half else flag
        box = side * half + slot % half
        out = sent_out if slot < half else kept_out
        out[slot % half] = merged(level, begin, size, kept_ref, got_ref, w_ref, box // 2, box)


def last_kernel(
    level, begin, size, order_ref, kept_ref, got_ref, joint_ref, after_ref, *outs
):
    half = kept_ref.shape[0]
    me = lax.axis_index("inner")
    width = joint_ref.shape[2]
    piece = outs[0].shape[2]
    pieces = joint_ref.shape[0] * width // piece
    per_box = joint_ref.shape[0] // (2 * half)
    for t in range(pieces // 2):
        for odd in range(2):
            out = outs[t].at[odd]
            first = jnp.bitwise_xor(me, 2 * t + odd) * (piece // width)
            for n in range(piece // width):
                k = order_ref[0, 0, (first + n) // per_box] // 2
                out[:, n * width : (n + 1) * width] = merged(
                    level, begin, size, kept_ref, got_ref, joint_ref, k, first + n
                )


def pack_kernel(*refs):
    out = refs[-1]
    for t in range(out.shape[0]):
        out[t] = refs[t][1]


def place_kernel(cuts, counts, *refs):
    out, held, sems = refs[-3:]
    rows = refs[0].shape[2]
    owners = out.shape[0] // rows
    me = lax.axis_index("inner")
    copies = []
    for step in range(owners):
        owner = jnp.bitwise_xor(me, step)
        window = pl.ds(pl.multiple_of(owner * rows, rows), rows)
        for n, (begin, size) in enumerate(cuts):
            chunk = refs[sum(counts[:n]) : sum(counts[: n + 1])]
            block = chunk[step // 2][0]
            if step % 2:
                late = [(ref, t) for ref in chunk[owners // 2 :] for t in range(ref.shape[0])]
                ref, t = late[step // 2]
                block = ref[t]
            held[step, :, begin : begin + size] = block.T
        copies += copy_all([pltpu.make_async_copy(held.at[step], out.at[window], sems.at[step])])
    for copy in copies:
        copy.wait()


def on_device(vectors, leaf_basis, transfer, core_mats, row_basis, box_order):
    boxes = transfer.shape[3]
    half = boxes // 2
    rank = leaf_basis.shape[1]
    columns = vectors.shape[1]
    levels = transfer.shape[0]
    inner = lax.axis_size("inner")
    piece = vectors.shape[0] // inner
    width = min(piece, vectors.shape[0] // boxes)
    edges = [columns * sum(PARTS[:n]) // sum(PARTS) for n in range(len(PARTS) + 1)]
    cuts = [(a, b - a) for a, b in zip(edges, edges[1:])]
    count = len(cuts)
    held = [None] * count
    done = [None] * count
    level_w = inside = joint = after = None

    for step in ORDER:
        kind, n = step[0], "abcdefgh".find(step[-1])
        if kind == "f":
            firsts = [cuts[0], (cuts[1][0], columns - cuts[1][0])]
            sent_a, kept_a, sent_b, kept_b = call(
                functools.partial(leaf_kernel, firsts),
                [arr(half, size, rank) for _, size in firsts for _ in range(2)],
                [vectors, leaf_basis],
                [HBM] * 2,
                [
                    pltpu.VMEM(vectors.shape, jnp.bfloat16),
                    pltpu.VMEM(leaf_basis.shape, jnp.bfloat16),
                    pltpu.SemaphoreType.DMA((2, boxes)),
                ],
                name="leaves",
                room=LEAF_ROOM,
            )
            got_a, got_b = swapped(sent_a, "inner", 1), swapped(sent_b, "inner", 1)
            held = [(kept_a, got_a, 0)]
            held += [(kept_b, got_b, begin - cuts[1][0]) for begin, _ in cuts[1:]]
            after = kept_b
        elif kind == "w":
            level_w = call(
                load_kernel,
                [arr(boxes, 2 * rank, rank)],
                [transfer, after],
                [HBM, ANY],
                [pltpu.SemaphoreType.DMA],
                name="weights",
                room=LOAD_ROOM,
            )[0]
            after = level_w
        elif kind == "i":
            inside = call(
                inside_kernel,
                [arr(vectors.shape[0] // width, rank, width)],
                [core_mats, row_basis, after],
                [VMEM, VMEM, ANY],
                name="inside",
            )[0]
            after = inside
        elif kind == "j":
            joint = call(
                functools.partial(join_kernel, levels - 1),
                [arr(vectors.shape[0] // width, 2 * rank, width)],
                [box_order, transfer, inside, after],
                [SMEM, VMEM, VMEM, ANY],
                name="join",
            )[0]
            after = joint
        elif kind == "m":
            level = int(step[1])
            size = cuts[n][1]
            kept, got, begin = held[n]
            sent, kept = call(
                functools.partial(merge_kernel, level, begin, size),
                [arr(half, size, rank)] * 2,
                [kept, got, transfer if level else level_w, after],
                [VMEM, VMEM, VMEM, ANY],
                name=f"merge{level}{step[-1]}",
            )
            after = kept
            axis, bit = level_axis(level + 1)
            held[n] = (kept, swapped(sent, axis, 1 << bit), 0)
        elif kind == "o":
            size = cuts[n][1]
            kept, got, begin = held[n]
            outs = call(
                functools.partial(last_kernel, levels - 1, begin, size),
                [arr(2, size, piece)] * (inner // 2),
                [box_order, kept, got, joint, after],
                [SMEM, VMEM, VMEM, VMEM, ANY],
                name=f"last{step[-1]}",
            )
            after = outs[0]
            sent = [None] * (inner // 2)
            for t in turns(inner // 2):
                sent[t] = swapped(outs[t], "inner", 2 * t)
            done[n] = [outs[0]] + sent[1:]
        elif kind in "qr":
            groups = [done[n]] if kind == "q" else [[x] for x in done[n]]
            for group in groups:
                after = call(
                    pack_kernel,
                    [arr(len(group), cuts[n][1], piece)],
                    group + [after],
                    [VMEM] * len(group) + [ANY],
                    name=f"pack{step[-1]}",
                )[0]
                done[n] = done[n] + [swapped(after, "inner", 1)]
    flat = [x for part in done for x in part]
    return call(
        functools.partial(place_kernel, cuts, [len(part) for part in done]),
        [arr(*vectors.shape)],
        flat,
        [VMEM] * len(flat),
        [
            pltpu.VMEM((inner, piece, columns), jnp.bfloat16),
            pltpu.SemaphoreType.DMA((inner,)),
        ],
        name="place",
        out_spec=HBM,
    )[0]


def solution(mesh):
    in_specs = (
        P(("outer", "inner"), None),
        P(("outer", "inner"), None),
        P(None, "outer", "inner", None, None, None),
        P("outer", "inner", None, None, None),
        P(("outer", "inner"), None),
        P("outer", "inner", None),
    )
    out_specs = P(("outer", "inner"), None)
    return jax.shard_map(
        on_device, mesh=mesh, in_specs=in_specs, out_specs=out_specs, check_vma=False
    )
```

```python
import functools

import jax
import jax.numpy as jnp
from jax import lax
from jax.experimental import pallas as pl
from jax.experimental.pallas import tpu as pltpu
from jax.sharding import PartitionSpec as P

INNER_LEVELS = 2
PARTS = (4, 5, 7)
COSTS = {"merge2c":.4,"lastb":.1,"lastc":.4,"packc":2,"lasta":1,"packa":2,"packb":1,"merge1b":.4,"join":.3,"inside":.3,"merge2a":.4,"merge1a":1,"place":5,"space":10}
ORDER = ("f", "w", "m0a", "m0b", "m0c", "i", "m1a", "m1b", "j", "m2a", "m1c", "m2b", "oa", "m2c", "ob", "qa", "oc", "qb", "uc", "x", "z", "tc")
LEAF_ROOM = 52
LOAD_ROOM = 48
HBM = pl.BlockSpec(memory_space=pltpu.HBM)
VMEM = pl.BlockSpec(memory_space=pltpu.VMEM)
ANY = pl.BlockSpec(memory_space=pl.ANY)
SMEM = pl.BlockSpec(memory_space=pltpu.SMEM)


def turns(count):
    return sorted(range(1, count), key=lambda t: (t < count // 2, t))


def swapped(array, axis, step):
    return lax.ppermute(array, axis, [(i, i ^ step) for i in range(lax.axis_size(axis))])


def level_axis(level):
    return ("inner", level) if level < INNER_LEVELS else ("outer", level - INNER_LEVELS)


def bit_of(level):
    axis, bit = level_axis(level)
    return jnp.bitwise_and(jnp.right_shift(lax.axis_index(axis), bit), 1)


def arr(*shape):
    return jax.ShapeDtypeStruct(shape, jnp.bfloat16)


def dot(a, b, dims=((1,), (0,))):
    return lax.dot_general(a, b, (dims, ((), ())), preferred_element_type=jnp.float32)


def call(kernel, outs, ins, specs, scratch=(), name=None, room=24, out_specs=None, aliases=None):
    run = pl.pallas_call(
        kernel,
        name=name,
        out_shape=outs,
        in_specs=specs,
        out_specs=out_specs or [VMEM] * len(outs),
        input_output_aliases=aliases or {},
        scratch_shapes=list(scratch),
        compiler_params=pltpu.CompilerParams(vmem_limit_bytes=room * 1024 * 1024),
        cost_estimate=pl.CostEstimate(
            flops=int(COSTS.get(name, 2) * 1e9), bytes_accessed=0, transcendentals=0
        ),
    )
    return list(run(*ins))


def copy_all(copies):
    for copy in copies:
        copy.start()
    return copies


def load_kernel(w_hbm, after_ref, w_out, sems):
    parts = sems.shape[0]
    each = w_out.shape[0] // parts
    loads = copy_all(
        [
            pltpu.make_async_copy(
                w_hbm.at[0, 0, 0, pl.ds(n * each, each)],
                w_out.at[pl.ds(n * each, each)],
                sems.at[n],
            )
            for n in range(parts)
        ]
    )
    for load in loads:
        load.wait()


def leaf_kernel(cuts, x_hbm, v_hbm, *refs):
    outs, (x_ref, v_ref, sems) = refs[:-3], refs[-3:]
    half = outs[0].shape[0]
    flag = bit_of(0)
    depth = x_ref.shape[1]
    rows = depth // half
    loads = []
    for late in range(2):
        side = flag if late else 1 - flag
        at = pl.ds(pl.multiple_of(side * depth, depth), depth)
        loads.append(
            copy_all(
                [
                    pltpu.make_async_copy(x_hbm.at[at], x_ref.at[late], sems.at[0, late]),
                    pltpu.make_async_copy(v_hbm.at[at], v_ref.at[late], sems.at[1, late]),
                ]
            )
        )
    for late in range(2):
        for load in loads[late]:
            load.wait()
        for slot in range(half):
            at = pl.ds(slot * rows, rows)
            state = dot(x_ref[late, at, :].T, v_ref[late, at, :]).astype(jnp.bfloat16)
            for n, (begin, size) in enumerate(cuts):
                outs[2 * n + late][slot] = state[begin : begin + size]


def inside_kernel(core_ref, u_ref, after_ref, out):
    width = out.shape[2]
    for n in range(out.shape[0]):
        box = n * width // (u_ref.shape[0] // core_ref.shape[2])
        inside = dot(core_ref[0, 0, box], u_ref[n * width : (n + 1) * width, :], ((1,), (1,)))
        out[n] = inside.astype(jnp.bfloat16)


def join_kernel(level, order_ref, w_ref, inside_ref, after_ref, out, slots_out):
    per_box = inside_ref.shape[0] // w_ref.shape[3]
    for box in range(slots_out.shape[0]):
        slots_out[box] = jnp.full(slots_out.shape[1:], order_ref[0, 0, box] // 2, jnp.int32)
    for n in range(out.shape[0]):
        joint = dot(w_ref[level, 0, 0, order_ref[0, 0, n // per_box]], inside_ref[n])
        out[n] = joint.astype(jnp.bfloat16)


def merged(level, begin, size, kept_ref, got_ref, w_ref, k, box):
    rank = kept_ref.shape[2]
    flag = bit_of(level)
    at = pl.ds(begin, size)
    place = (level, 0, 0, box) if len(w_ref.shape) == 6 else (box,)
    mine = w_ref[(*place, pl.ds(pl.multiple_of(flag * rank, rank), rank), slice(None))]
    other = w_ref[(*place, pl.ds(pl.multiple_of((1 - flag) * rank, rank), rank), slice(None))]
    total = dot(kept_ref[k, at, :], mine) + dot(got_ref[k, at, :], other)
    return total.astype(jnp.bfloat16)


def merge_kernel(level, begin, size, kept_ref, got_ref, w_ref, after_ref, sent_out, kept_out):
    half = kept_ref.shape[0]
    flag = bit_of(level + 1)
    for slot in range(2 * half):
        side = 1 - flag if slot < half else flag
        box = side * half + slot % half
        out = sent_out if slot < half else kept_out
        out[slot % half] = merged(level, begin, size, kept_ref, got_ref, w_ref, box // 2, box)


def last_kernel(
    level, begin, size, slots_ref, kept_ref, got_ref, joint_ref, after_ref, *outs
):
    half = kept_ref.shape[0]
    me = lax.axis_index("inner")
    width = joint_ref.shape[2]
    piece = outs[0].shape[2]
    pieces = joint_ref.shape[0] * width // piece
    per_box = joint_ref.shape[0] // (2 * half)
    for t in range(pieces // 2):
        for odd in range(2):
            out = outs[t].at[odd]
            first = jnp.bitwise_xor(me, 2 * t + odd) * (piece // width)
            for n in range(piece // width):
                k = jnp.max(slots_ref[(first + n) // per_box])
                out[:, n * width : (n + 1) * width] = merged(
                    level, begin, size, kept_ref, got_ref, joint_ref, k, first + n
                )


def pack_kernel(*refs):
    out = refs[-1]
    for t in range(out.shape[0]):
        out[t] = refs[t][1]


def space_kernel(after_ref, out):
    out[...] = jnp.zeros_like(out)


def place_kernel(cuts, counts, early, *refs):
    out, held_out, held, sems = refs[-4:]
    rows = refs[0].shape[2]
    owners = out.shape[0] // rows
    me = lax.axis_index("inner")
    copies = []
    for step in range(owners):
        whole = step < 2 * early
        block_out = held.at[step] if whole else held_out.at[step - 2 * early]
        for n, (begin, size) in enumerate(cuts[: None if whole else -1]):
            at = sum(counts[:n])
            chunk = refs[at : at + counts[n]]
            block = chunk[step // 2][0]
            if step % 2:
                mine = early if n == len(cuts) - 1 else owners // 2
                late = [(ref, t) for ref in chunk[mine:] for t in range(ref.shape[0])]
                ref, t = late[step // 2]
                block = ref[t]
            block_out[:, begin : begin + size] = block.T
        if whole:
            owner = jnp.bitwise_xor(me, step)
            window = pl.ds(pl.multiple_of(owner * rows, rows), rows)
            copies += copy_all(
                [pltpu.make_async_copy(held.at[step], out.at[window], sems.at[step])]
            )
    for copy in copies:
        copy.wait()


def finish_kernel(cut, first_ref, held_ref, *refs):
    even_refs, (odd_ref, out, held, sems) = refs[:-4], refs[-4:]
    begin, size = cut
    rows = held.shape[1]
    late = held.shape[0]
    first = out.shape[0] // rows - late
    me = lax.axis_index("inner")
    copies = []
    for step in range(late):
        block = odd_ref[step // 2] if step % 2 else even_refs[step // 2][0]
        held[step] = held_ref[step]
        held[step, :, begin : begin + size] = block.T
        owner = jnp.bitwise_xor(me, first + step)
        window = pl.ds(pl.multiple_of(owner * rows, rows), rows)
        copies += copy_all([pltpu.make_async_copy(held.at[step], out.at[window], sems.at[step])])
    for copy in copies:
        copy.wait()


def on_device(vectors, leaf_basis, transfer, core_mats, row_basis, box_order):
    boxes = transfer.shape[3]
    half = boxes // 2
    rank = leaf_basis.shape[1]
    columns = vectors.shape[1]
    levels = transfer.shape[0]
    inner = lax.axis_size("inner")
    piece = vectors.shape[0] // inner
    width = min(piece, vectors.shape[0] // boxes)
    edges = [columns * sum(PARTS[:n]) // sum(PARTS) for n in range(len(PARTS) + 1)]
    cuts = [(a, b - a) for a, b in zip(edges, edges[1:])]
    count = len(cuts)
    held = [None] * count
    done = [None] * count
    swaps = [[] for _ in cuts]
    early = inner // 4
    level_w = inside = joint = after = None

    for step in ORDER:
        kind, n = step[0], "abcdefgh".find(step[-1])
        if kind == "f":
            firsts = [cuts[0], (cuts[1][0], columns - cuts[1][0])]
            sent_a, kept_a, sent_b, kept_b = call(
                functools.partial(leaf_kernel, firsts),
                [arr(half, size, rank) for _, size in firsts for _ in range(2)],
                [vectors, leaf_basis],
                [HBM] * 2,
                [
                    pltpu.VMEM((2, vectors.shape[0] // 2, columns), jnp.bfloat16),
                    pltpu.VMEM((2, vectors.shape[0] // 2, rank), jnp.bfloat16),
                    pltpu.SemaphoreType.DMA((2, 2)),
                ],
                name="leaves",
                room=LEAF_ROOM,
            )
            got_a, got_b = swapped(sent_a, "inner", 1), swapped(sent_b, "inner", 1)
            held = [(kept_a, got_a, 0)]
            held += [(kept_b, got_b, begin - cuts[1][0]) for begin, _ in cuts[1:]]
            after = kept_b
        elif kind == "w":
            level_w = call(
                load_kernel,
                [arr(boxes, 2 * rank, rank)],
                [transfer, after],
                [HBM, ANY],
                [pltpu.SemaphoreType.DMA((2,))],
                name="weights",
                room=LOAD_ROOM,
            )[0]
            after = level_w
        elif kind == "i":
            inside = call(
                inside_kernel,
                [arr(vectors.shape[0] // width, rank, width)],
                [core_mats, row_basis, after],
                [VMEM, VMEM, ANY],
                name="inside",
            )[0]
            after = inside
        elif kind == "j":
            joint, slots = call(
                functools.partial(join_kernel, levels - 1),
                [
                    arr(vectors.shape[0] // width, 2 * rank, width),
                    jax.ShapeDtypeStruct((boxes, 8, 128), jnp.int32),
                ],
                [box_order, transfer, inside, after],
                [SMEM, VMEM, VMEM, ANY],
                name="join",
            )
            after = joint
        elif kind == "m":
            level = int(step[1])
            size = cuts[n][1]
            kept, got, begin = held[n]
            sent, kept = call(
                functools.partial(merge_kernel, level, begin, size),
                [arr(half, size, rank)] * 2,
                [kept, got, transfer if level else level_w, after],
                [VMEM, VMEM, VMEM, ANY],
                name=f"merge{level}{step[-1]}",
            )
            after = kept
            axis, bit = level_axis(level + 1)
            held[n] = (kept, swapped(sent, axis, 1 << bit), 0)
        elif kind == "o":
            size = cuts[n][1]
            kept, got, begin = held[n]
            outs = call(
                functools.partial(last_kernel, levels - 1, begin, size),
                [arr(2, size, piece)] * (inner // 2),
                [slots, kept, got, joint, after],
                [VMEM, VMEM, VMEM, VMEM, ANY],
                name=f"last{step[-1]}",
            )
            after = outs[0]
            sent = [outs[0]] + [None] * (inner // 2 - 1)
            for t in turns(inner // 2):
                sent[t] = swapped(outs[t], "inner", 2 * t)
            done[n] = sent
        elif kind == "x":
            after = call(space_kernel, [arr(16, 128)], [after], [ANY], name="space")[0]
        elif kind in "qut":
            pairs = inner // 2
            begin = early if kind == "t" else 0
            end = early if kind == "u" else pairs
            if begin < end:
                group = done[n][begin:end]
                after = call(
                    pack_kernel,
                    [arr(len(group), cuts[n][1], piece)],
                    group + [after],
                    [VMEM] * len(group) + [ANY],
                    name=f"pack{step[-1]}",
                )[0]
                swaps[n].append(swapped(after, "inner", 1))
        elif kind == "z":
            counts = [len(a) + len(b) for a, b in zip(done[:-1], swaps)] + [early + 1]
            flat = [x for n in range(count - 1) for x in done[n] + swaps[n]]
            flat += done[-1][:early] + swaps[-1]
            placed, rest = call(
                functools.partial(place_kernel, cuts, counts, early),
                [arr(*vectors.shape), arr(inner - 2 * early, piece, columns)],
                flat + [after],
                [VMEM] * len(flat) + [ANY],
                [
                    pltpu.VMEM((2 * early, piece, columns), jnp.bfloat16),
                    pltpu.SemaphoreType.DMA((2 * early,)),
                ],
                name="place",
                out_specs=[HBM, VMEM],
            )
            after = rest
    flat = done[-1][early:] + swaps[-1][-1:]
    return call(
        functools.partial(finish_kernel, cuts[-1]),
        [arr(*vectors.shape)],
        [placed, rest, *flat],
        [HBM, VMEM] + [VMEM] * len(flat),
        [
            pltpu.VMEM((inner - 2 * early, piece, columns), jnp.bfloat16),
            pltpu.SemaphoreType.DMA((inner - 2 * early,)),
        ],
        name="finish",
        out_specs=[HBM],
        aliases={0: 0},
    )[0]


def solution(mesh):
    in_specs = (
        P(("outer", "inner"), None),
        P(("outer", "inner"), None),
        P(None, "outer", "inner", None, None, None),
        P("outer", "inner", None, None, None),
        P(("outer", "inner"), None),
        P("outer", "inner", None),
    )
    out_specs = P(("outer", "inner"), None)
    return jax.shard_map(
        on_device, mesh=mesh, in_specs=in_specs, out_specs=out_specs, check_vma=False
    )
```

```python
import functools

import jax
import jax.numpy as jnp
from jax import lax
from jax.experimental import pallas as pl
from jax.experimental.pallas import tpu as pltpu
from jax.sharding import PartitionSpec as P

INNER_LEVELS = 2
PARTS = (4, 6, 6)
GROUPS = ("a", "b", "c")
XS = 1
TURN = 1
COSTS = {
    "merge2c": 1,
    "lastb": 0.1,
    "lastc": 10,
    "packc": 10,
    "lasta": 1,
    "packa": 5,
    "packb": 10,
    "merge1b": 0.4,
    "join": 0.3,
    "inside": 0.3,
    "merge2a": 0.4,
    "merge1a": 1,
    "place": 10,
    "space": 10,
    "merge1c": 1,
    "weights": 1,
    "merge0a": 10,
    "farc": 0.4,
    "couplec": 10,
    "holda": 5,
}
ORDER = (
    "f",
    "w",
    "m0a",
    "m0c",
    "m0b",
    "i",
    "m1a",
    "m1b",
    "m2a",
    "j",
    "m1c",
    "m2b",
    "oa",
    "m2c",
    "ob",
    "ya",
    "efc",
    "onc",
    "pc",
    "qa",
    "qb",
    "uc",
    "x",
    "z",
)
LEAF_ROOM = 52
LOAD_ROOM = 48
HBM = pl.BlockSpec(memory_space=pltpu.HBM)
VMEM = pl.BlockSpec(memory_space=pltpu.VMEM)
ANY = pl.BlockSpec(memory_space=pl.ANY)
SMEM = pl.BlockSpec(memory_space=pltpu.SMEM)


def swapped(array, axis, step):
    return lax.ppermute(array, axis, [(i, i ^ step) for i in range(lax.axis_size(axis))])


def level_axis(level):
    return ("inner", level) if level < INNER_LEVELS else ("outer", level - INNER_LEVELS)


def bit_of(level):
    axis, bit = level_axis(level)
    return jnp.bitwise_and(jnp.right_shift(lax.axis_index(axis), bit), 1)


def arr(*shape):
    return jax.ShapeDtypeStruct(shape, jnp.bfloat16)


def dot(a, b, dims=((1,), (0,))):
    return lax.dot_general(a, b, (dims, ((), ())), preferred_element_type=jnp.float32)


def call(kernel, outs, ins, specs, scratch=(), name=None, room=24, out_specs=None, aliases=None):
    run = pl.pallas_call(
        kernel,
        name=name,
        out_shape=outs,
        in_specs=specs,
        out_specs=out_specs or [VMEM] * len(outs),
        input_output_aliases=aliases or {},
        scratch_shapes=list(scratch),
        compiler_params=pltpu.CompilerParams(vmem_limit_bytes=room * 1024 * 1024),
        cost_estimate=pl.CostEstimate(
            flops=int(COSTS.get(name, 2) * 1e9), bytes_accessed=0, transcendentals=0
        ),
    )
    return list(run(*ins))


def copy_all(copies):
    for copy in copies:
        copy.start()
    return copies


def load_kernel(w_hbm, after_ref, w_out, sems):
    parts = sems.shape[0]
    each = w_out.shape[0] // parts
    loads = copy_all(
        [
            pltpu.make_async_copy(
                w_hbm.at[0, 0, 0, pl.ds(n * each, each)],
                w_out.at[pl.ds(n * each, each)],
                sems.at[n],
            )
            for n in range(parts)
        ]
    )
    for load in loads:
        load.wait()


def leaf_kernel(cuts, x_hbm, v_hbm, *refs):
    outs, (x_ref, v_ref, sems) = refs[:-3], refs[-3:]
    half = outs[0].shape[0]
    flag = bit_of(0)
    depth = x_ref.shape[1]
    rows = depth // half
    loads = []
    for late in range(2):
        side = flag if late else 1 - flag
        at = pl.ds(pl.multiple_of(side * depth, depth), depth)
        loads.append(
            copy_all(
                [
                    pltpu.make_async_copy(x_hbm.at[at], x_ref.at[late], sems.at[0, late]),
                    pltpu.make_async_copy(v_hbm.at[at], v_ref.at[late], sems.at[1, late]),
                ]
            )
        )
    for late in range(2):
        for load in loads[late]:
            load.wait()
        for slot in range(half):
            at = pl.ds(slot * rows, rows)
            state = dot(x_ref[late, at, :].T, v_ref[late, at, :]).astype(jnp.bfloat16)
            for n, (begin, size) in enumerate(cuts):
                outs[2 * n + late][slot] = state[begin : begin + size]


def inside_kernel(core_ref, u_ref, after_ref, out):
    width = out.shape[2]
    for n in range(out.shape[0]):
        box = n * width // (u_ref.shape[0] // core_ref.shape[2])
        inside = dot(core_ref[0, 0, box], u_ref[n * width : (n + 1) * width, :], ((1,), (1,)))
        out[n] = inside.astype(jnp.bfloat16)


def join_kernel(level, order_ref, w_ref, inside_ref, after_ref, out, slots_out):
    per_box = inside_ref.shape[0] // w_ref.shape[3]
    for box in range(slots_out.shape[0]):
        slots_out[box] = jnp.full(slots_out.shape[1:], order_ref[0, 0, box] // 2, jnp.int32)
    for n in range(out.shape[0]):
        joint = dot(w_ref[level, 0, 0, order_ref[0, 0, n // per_box]], inside_ref[n])
        out[n] = joint.astype(jnp.bfloat16)


def merged(level, begin, size, kept_ref, got_ref, w_ref, k, box):
    rank = kept_ref.shape[2]
    flag = bit_of(level)
    at = pl.ds(begin, size)
    place = (level, 0, 0, box) if len(w_ref.shape) == 6 else (box,)
    mine = w_ref[(*place, pl.ds(pl.multiple_of(flag * rank, rank), rank), slice(None))]
    other = w_ref[(*place, pl.ds(pl.multiple_of((1 - flag) * rank, rank), rank), slice(None))]
    total = dot(kept_ref[k, at, :], mine) + dot(got_ref[k, at, :], other)
    return total.astype(jnp.bfloat16)


def merge_kernel(level, begin, size, kept_ref, got_ref, w_ref, after_ref, sent_out, kept_out):
    half = kept_ref.shape[0]
    flag = bit_of(level + 1)
    for slot in range(2 * half):
        side = 1 - flag if slot < half else flag
        box = side * half + slot % half
        out = sent_out if slot < half else kept_out
        out[slot % half] = merged(level, begin, size, kept_ref, got_ref, w_ref, box // 2, box)


def last_kernel(level, pairs, apart, parts, slots_ref, joint_ref, after_ref, *refs):
    states, outs = refs[: 2 * len(parts)], refs[2 * len(parts) :]
    half = states[0].shape[0]
    me = lax.axis_index("inner")
    width = joint_ref.shape[2]
    piece = outs[0].shape[2]
    per_box = joint_ref.shape[0] // (2 * half)
    for at, t in enumerate(pairs):
        for odd in range(2):
            out = outs[odd].at[at] if apart else outs[at].at[odd]
            first = jnp.bitwise_xor(me, 2 * t + odd) * (piece // width)
            for n in range(piece // width):
                k = jnp.max(slots_ref[(first + n) // per_box])
                row = 0
                for i, (begin, size) in enumerate(parts):
                    kept_ref, got_ref = states[2 * i : 2 * i + 2]
                    out[row : row + size, n * width : (n + 1) * width] = merged(
                        level, begin, size, kept_ref, got_ref, joint_ref, k, first + n
                    )
                    row += size


def couple_kernel(mine_ref, got_ref, after_ref, *outs):
    for t, out in enumerate(outs):
        out[0] = mine_ref[t]
        out[1] = got_ref[t]


def pack_kernel(turns, *refs):
    out = refs[-1]
    for at, t in enumerate(turns):
        out[t] = refs[at][1]


def space_kernel(*refs):
    refs[-1][...] = jnp.zeros_like(refs[-1])


def place_kernel(cuts, counts, early, *refs):
    out, held_out, held, sems = refs[-4:]
    rows = refs[0].shape[2]
    owners = out.shape[0] // rows
    me = lax.axis_index("inner")
    copies = []
    for step in range(owners):
        whole = step < 2 * early
        block_out = held.at[step] if whole else held_out.at[step - 2 * early]
        for n, (begin, size) in enumerate(cuts[: None if whole else -1]):
            at = sum(counts[:n])
            chunk = refs[at : at + counts[n]]
            block = chunk[step // 2][0]
            if step % 2:
                mine = early if n == len(cuts) - 1 else owners // 2
                late = [(ref, t) for ref in chunk[mine:] for t in range(ref.shape[0])]
                ref, t = late[step // 2]
                block = ref[t]
            block_out[:, begin : begin + size] = block.T
        if whole:
            owner = jnp.bitwise_xor(me, step)
            window = pl.ds(pl.multiple_of(owner * rows, rows), rows)
            copies += copy_all(
                [pltpu.make_async_copy(held.at[step], out.at[window], sems.at[step])]
            )
    for copy in copies:
        copy.wait()


def finish_kernel(cut, first_ref, held_ref, *refs):
    blocks, (out, held, sems) = refs[:-3], refs[-3:]
    begin, size = cut
    rows = held.shape[1]
    late = held.shape[0]
    first = out.shape[0] // rows - late
    me = lax.axis_index("inner")
    copies = []
    for step in range(late):
        block = blocks[step // 2][step % 2]
        if step % 2 and len(blocks) > late // 2:
            block = blocks[-1][step // 2]
        held[step] = held_ref[step]
        held[step, :, begin : begin + size] = block.T
        owner = jnp.bitwise_xor(me, first + step)
        window = pl.ds(pl.multiple_of(owner * rows, rows), rows)
        copies += copy_all([pltpu.make_async_copy(held.at[step], out.at[window], sems.at[step])])
    for copy in copies:
        copy.wait()


def on_device(vectors, leaf_basis, transfer, core_mats, row_basis, box_order):
    boxes = transfer.shape[3]
    half = boxes // 2
    rank = leaf_basis.shape[1]
    columns = vectors.shape[1]
    levels = transfer.shape[0]
    inner = lax.axis_size("inner")
    piece = vectors.shape[0] // inner
    width = min(piece, vectors.shape[0] // boxes)
    edges = [columns * sum(PARTS[:n]) // sum(PARTS) for n in range(len(PARTS) + 1)]
    cuts = [(a, b - a) for a, b in zip(edges, edges[1:])]
    count = len(cuts)
    groups = [["abcdefgh".index(x) for x in names] for names in GROUPS]
    spans = [(cuts[m[0]][0], sum(cuts[x][1] for x in m)) for m in groups]
    held = [None] * count
    done = [[None] * (inner // 2) for _ in groups]
    swaps = [[] for _ in groups]
    early = inner // 4
    level_w = inside = joint = after = None

    for step in ORDER:
        kind, n = step[0], "abcdefgh".find(step[-1])
        g = [names[0] for names in GROUPS].index(step[-1]) if kind in "oqutepy" else 0
        if kind == "f":
            firsts = [cuts[0], (cuts[1][0], columns - cuts[1][0])]
            sent_a, kept_a, sent_b, kept_b = call(
                functools.partial(leaf_kernel, firsts),
                [arr(half, size, rank) for _, size in firsts for _ in range(2)],
                [vectors, leaf_basis],
                [HBM] * 2,
                [
                    pltpu.VMEM((2, vectors.shape[0] // 2, columns), jnp.bfloat16),
                    pltpu.VMEM((2, vectors.shape[0] // 2, rank), jnp.bfloat16),
                    pltpu.SemaphoreType.DMA((2, 2)),
                ],
                name="leaves",
                room=LEAF_ROOM,
            )
            got_a, got_b = swapped(sent_a, "inner", 1), swapped(sent_b, "inner", 1)
            held = [(kept_a, got_a, 0)]
            held += [(kept_b, got_b, begin - cuts[1][0]) for begin, _ in cuts[1:]]
            after = kept_b
        elif kind == "w":
            level_w = call(
                load_kernel,
                [arr(boxes, 2 * rank, rank)],
                [transfer, after],
                [HBM, ANY],
                [pltpu.SemaphoreType.DMA((2,))],
                name="weights",
                room=LOAD_ROOM,
            )[0]
            after = level_w
        elif kind == "i":
            inside = call(
                inside_kernel,
                [arr(vectors.shape[0] // width, rank, width)],
                [core_mats, row_basis, after],
                [VMEM, VMEM, ANY],
                name="inside",
            )[0]
            after = inside
        elif kind == "j":
            joint, slots = call(
                functools.partial(join_kernel, levels - 1),
                [
                    arr(vectors.shape[0] // width, 2 * rank, width),
                    jax.ShapeDtypeStruct((boxes, 8, 128), jnp.int32),
                ],
                [box_order, transfer, inside, after],
                [SMEM, VMEM, VMEM, ANY],
                name="join",
            )
            after = joint
        elif kind == "m":
            level = int(step[1])
            size = cuts[n][1]
            kept, got, begin = held[n]
            sent, kept = call(
                functools.partial(merge_kernel, level, begin, size),
                [arr(half, size, rank)] * 2,
                [kept, got, transfer if level else level_w, after],
                [VMEM, VMEM, VMEM, ANY],
                name=f"merge{level}{step[-1]}",
            )
            after = kept
            axis, bit = level_axis(level + 1)
            held[n] = (kept, swapped(sent, axis, 1 << bit), 0)
        elif kind in "oe":
            apart = kind == "e"
            near = step[1] == "n"
            pairs = range(early if apart else 0, early if near else inner // 2)
            members = groups[g]
            size = spans[g][1]
            states = [x for m in members for x in held[m][:2]]
            outs = call(
                functools.partial(
                    last_kernel,
                    levels - 1,
                    pairs,
                    apart,
                    [(held[m][2], cuts[m][1]) for m in members],
                ),
                [arr(len(pairs), size, piece)] * 2 if apart else [arr(2, size, piece)] * len(pairs),
                [slots, joint, after, *states],
                [VMEM, VMEM, ANY] + [VMEM] * len(states),
                name=("far" if apart else "last") + step[-1],
            )
            after = outs[0]
            if apart:
                coupled = [outs[0], swapped(outs[1], "inner", 1)]
            else:
                for t, x in zip(pairs, outs):
                    done[g][t] = swapped(x, "inner", 2 * t) if t else x
        elif kind == "p":
            outs = call(
                couple_kernel,
                [arr(2, spans[g][1], piece)] * (inner // 2 - early),
                coupled + [after],
                [VMEM, VMEM, ANY],
                name=f"couple{step[-1]}",
            )
            after = outs[0]
            for t, x in enumerate(outs, early):
                done[g][t] = swapped(x, "inner", 2 * t)
        elif kind == "y":
            after = call(
                space_kernel, [arr(16, 128)], [after, *done[g]], [ANY] * (1 + len(done[g])), name=f"hold{step[-1]}"
            )[0]
        elif kind == "x":
            first = [x for part in (swaps[:-2] if XS else []) for x in part]
            after = call(
                space_kernel, [arr(16, 128)], [after, *first], [ANY] * (1 + len(first)), name="space"
            )[0]
        elif kind in "qut":
            pairs = inner // 2
            begin = early if kind == "t" else 0
            end = early if kind == "u" else pairs
            if begin < end:
                turns = list(range(end - begin))
                if TURN:
                    turns = turns[early:] + turns[:early]
                group = [done[g][begin + t] for t in turns]
                after = call(
                    functools.partial(pack_kernel, turns),
                    [arr(len(group), spans[g][1], piece)],
                    group + [after],
                    [VMEM] * len(group) + [ANY],
                    name=f"pack{step[-1]}",
                )[0]
                swaps[g].append(swapped(after, "inner", 1))
        elif kind == "z":
            counts = [len(a) + len(b) for a, b in zip(done[:-1], swaps)] + [early + 1]
            flat = [x for d, w in zip(done[:-1], swaps) for x in d + w]
            flat += done[-1][:early] + swaps[-1][:1]
            placed, rest = call(
                functools.partial(place_kernel, spans, counts, early),
                [arr(*vectors.shape), arr(inner - 2 * early, piece, columns)],
                flat + [after],
                [VMEM] * len(flat) + [ANY],
                [
                    pltpu.VMEM((2 * early, piece, columns), jnp.bfloat16),
                    pltpu.SemaphoreType.DMA((2 * early,)),
                ],
                name="place",
                out_specs=[HBM, VMEM],
            )
            after = rest
    flat = done[-1][early:] + swaps[-1][1:]
    return call(
        functools.partial(finish_kernel, spans[-1]),
        [arr(*vectors.shape)],
        [placed, rest, *flat],
        [HBM, VMEM] + [VMEM] * len(flat),
        [
            pltpu.VMEM((inner - 2 * early, piece, columns), jnp.bfloat16),
            pltpu.SemaphoreType.DMA((inner - 2 * early,)),
        ],
        name="finish",
        out_specs=[HBM],
        aliases={0: 0},
    )[0]


def solution(mesh):
    in_specs = (
        P(("outer", "inner"), None),
        P(("outer", "inner"), None),
        P(None, "outer", "inner", None, None, None),
        P("outer", "inner", None, None, None),
        P(("outer", "inner"), None),
        P("outer", "inner", None),
    )
    out_specs = P(("outer", "inner"), None)
    return jax.shard_map(
        on_device, mesh=mesh, in_specs=in_specs, out_specs=out_specs, check_vma=False
    )
```

```python
import functools

import jax
import jax.numpy as jnp
from jax import lax
from jax.experimental import pallas as pl
from jax.experimental.pallas import tpu as pltpu
from jax.sharding import PartitionSpec as P

INNER_LEVELS = 2
PARTS = (4, 6, 6)
GROUPS = ("a", "b", "c")
COSTS = {
    "merge2c": 1,
    "lastb": 0.1,
    "lastc": 10,
    "packc": 10,
    "lasta": 1,
    "packa": 10,
    "packb": 10,
    "merge1b": 0.4,
    "join": 0.3,
    "inside": 0.1,
    "merge2a": 0.4,
    "merge1a": 1,
    "place": 10,
    "space": 10,
    "merge1c": 1,
    "weights": 1,
    "merge0a": 10,
    "nearc": 10,
    "farc": 0.4,
    "couplec": 10,
    "holda": 5,
    "sent0a": 5,
    "kept0a": 5,
    "sent1a": 0.5,
    "kept1a": 0.5,
}
ORDER = (
    "f",
    "w",
    "s0a",
    "k0a",
    "m0b",
    "m0c",
    "i",
    "s1a",
    "k1a",
    "m1b",
    "m2a",
    "j",
    "m1c",
    "m2b",
    "oa",
    "m2c",
    "ob",
    "ya",
    "efc",
    "onc",
    "pc",
    "qa",
    "qb",
    "uc",
    "x",
    "z",
)
LEAF_ROOM = 52
LOAD_ROOM = 48
HBM = pl.BlockSpec(memory_space=pltpu.HBM)
VMEM = pl.BlockSpec(memory_space=pltpu.VMEM)
ANY = pl.BlockSpec(memory_space=pl.ANY)
SMEM = pl.BlockSpec(memory_space=pltpu.SMEM)


def swapped(array, axis, step):
    return lax.ppermute(array, axis, [(i, i ^ step) for i in range(lax.axis_size(axis))])


def level_axis(level):
    return ("inner", level) if level < INNER_LEVELS else ("outer", level - INNER_LEVELS)


def bit_of(level):
    axis, bit = level_axis(level)
    return jnp.bitwise_and(jnp.right_shift(lax.axis_index(axis), bit), 1)


def arr(*shape):
    return jax.ShapeDtypeStruct(shape, jnp.bfloat16)


def dot(a, b, dims=((1,), (0,))):
    return lax.dot_general(a, b, (dims, ((), ())), preferred_element_type=jnp.float32)


def call(kernel, outs, ins, specs, scratch=(), name=None, room=24, out_specs=None, aliases=None):
    run = pl.pallas_call(
        kernel,
        name=name,
        out_shape=outs,
        in_specs=specs,
        out_specs=out_specs or [VMEM] * len(outs),
        input_output_aliases=aliases or {},
        scratch_shapes=list(scratch),
        compiler_params=pltpu.CompilerParams(vmem_limit_bytes=room * 1024 * 1024),
        cost_estimate=pl.CostEstimate(
            flops=int(COSTS.get(name, 2) * 1e9), bytes_accessed=0, transcendentals=0
        ),
    )
    return list(run(*ins))


def copy_all(copies):
    for copy in copies:
        copy.start()
    return copies


def load_kernel(w_hbm, after_ref, w_out, sems):
    parts = sems.shape[0]
    each = w_out.shape[0] // parts
    loads = copy_all(
        [
            pltpu.make_async_copy(
                w_hbm.at[0, 0, 0, pl.ds(n * each, each)],
                w_out.at[pl.ds(n * each, each)],
                sems.at[n],
            )
            for n in range(parts)
        ]
    )
    for load in loads:
        load.wait()


def leaf_kernel(cuts, x_hbm, v_hbm, *refs):
    outs, (x_ref, v_ref, sems) = refs[:-3], refs[-3:]
    half = outs[0].shape[0]
    flag = bit_of(0)
    depth = x_ref.shape[1]
    rows = depth // half
    loads = []
    for late in range(2):
        side = flag if late else 1 - flag
        at = pl.ds(pl.multiple_of(side * depth, depth), depth)
        loads.append(
            copy_all(
                [
                    pltpu.make_async_copy(x_hbm.at[at], x_ref.at[late], sems.at[0, late]),
                    pltpu.make_async_copy(v_hbm.at[at], v_ref.at[late], sems.at[1, late]),
                ]
            )
        )
    for late in range(2):
        for load in loads[late]:
            load.wait()
        for slot in range(half):
            at = pl.ds(slot * rows, rows)
            state = dot(x_ref[late, at, :].T, v_ref[late, at, :]).astype(jnp.bfloat16)
            for n, (begin, size) in enumerate(cuts):
                outs[2 * n + late][slot] = state[begin : begin + size]


def inside_kernel(core_ref, u_ref, after_ref, out):
    width = out.shape[2]
    for n in range(out.shape[0]):
        box = n * width // (u_ref.shape[0] // core_ref.shape[2])
        inside = dot(core_ref[0, 0, box], u_ref[n * width : (n + 1) * width, :], ((1,), (1,)))
        out[n] = inside.astype(jnp.bfloat16)


def join_kernel(level, order_ref, w_ref, inside_ref, after_ref, out, slots_out):
    per_box = inside_ref.shape[0] // w_ref.shape[3]
    for box in range(slots_out.shape[0]):
        slots_out[box] = jnp.full(slots_out.shape[1:], order_ref[0, 0, box] // 2, jnp.int32)
    for n in range(out.shape[0]):
        joint = dot(w_ref[level, 0, 0, order_ref[0, 0, n // per_box]], inside_ref[n])
        out[n] = joint.astype(jnp.bfloat16)


def merged(level, begin, size, kept_ref, got_ref, w_ref, k, box):
    rank = kept_ref.shape[2]
    flag = bit_of(level)
    at = pl.ds(begin, size)
    place = (level, 0, 0, box) if len(w_ref.shape) == 6 else (box,)
    mine = w_ref[(*place, pl.ds(pl.multiple_of(flag * rank, rank), rank), slice(None))]
    other = w_ref[(*place, pl.ds(pl.multiple_of((1 - flag) * rank, rank), rank), slice(None))]
    total = dot(kept_ref[k, at, :], mine) + dot(got_ref[k, at, :], other)
    return total.astype(jnp.bfloat16)


def merge_kernel(level, begin, size, sides, kept_ref, got_ref, w_ref, after_ref, *outs):
    half = kept_ref.shape[0]
    flag = bit_of(level + 1)
    for side, out in zip(sides, outs):
        for slot in range(half):
            box = (flag if side else 1 - flag) * half + slot
            out[slot] = merged(level, begin, size, kept_ref, got_ref, w_ref, box // 2, box)


def last_kernel(level, pairs, apart, parts, slots_ref, joint_ref, after_ref, *refs):
    states, outs = refs[: 2 * len(parts)], refs[2 * len(parts) :]
    half = states[0].shape[0]
    me = lax.axis_index("inner")
    width = joint_ref.shape[2]
    piece = outs[0].shape[2]
    per_box = joint_ref.shape[0] // (2 * half)
    for at, t in enumerate(pairs):
        for odd in range(2):
            if apart:
                out = outs[odd].at[at]
            else:
                out = outs[at].at[odd]
            first = jnp.bitwise_xor(me, 2 * t + odd) * (piece // width)
            for n in range(piece // width):
                k = jnp.max(slots_ref[(first + n) // per_box])
                row = 0
                for i, (begin, size) in enumerate(parts):
                    kept_ref, got_ref = states[2 * i : 2 * i + 2]
                    out[row : row + size, n * width : (n + 1) * width] = merged(
                        level, begin, size, kept_ref, got_ref, joint_ref, k, first + n
                    )
                    row += size


def couple_kernel(mine_ref, got_ref, after_ref, *outs):
    for t, out in enumerate(outs):
        out[0] = mine_ref[t]
        out[1] = got_ref[t]


def pack_kernel(turns, bases, *refs):
    out = refs[-1]
    for at, t in enumerate(turns):
        out[t] = refs[at][bases[at] + 1]


def space_kernel(*refs):
    refs[-1][...] = jnp.zeros_like(refs[-1])


def place_kernel(cuts, counts, early, turns, bases, *refs):
    out, held_out, held, sems = refs[-4:]
    rows = refs[0].shape[2]
    owners = out.shape[0] // rows
    me = lax.axis_index("inner")
    copies = []
    for step in range(owners):
        whole = step < 2 * early
        block_out = held.at[step] if whole else held_out.at[step - 2 * early]
        for n, (begin, size) in enumerate(cuts[: None if whole else -1]):
            at = sum(counts[:n])
            chunk = refs[at : at + counts[n]]
            block = chunk[turns.index(step // 2) if n < len(cuts) - 1 else step // 2][
                bases[n][step // 2]
            ]
            if step % 2:
                mine = early if n == len(cuts) - 1 else owners // 2
                late = [(ref, t) for ref in chunk[mine:] for t in range(ref.shape[0])]
                ref, t = late[step // 2]
                block = ref[t]
            block_out[:, begin : begin + size] = block.T
        if whole:
            owner = jnp.bitwise_xor(me, step)
            window = pl.ds(pl.multiple_of(owner * rows, rows), rows)
            copies += copy_all(
                [pltpu.make_async_copy(held.at[step], out.at[window], sems.at[step])]
            )
    for copy in copies:
        copy.wait()


def finish_kernel(cut, first_ref, held_ref, *refs):
    blocks, (out, held, sems) = refs[:-3], refs[-3:]
    begin, size = cut
    rows = held.shape[1]
    late = held.shape[0]
    first = out.shape[0] // rows - late
    me = lax.axis_index("inner")
    copies = []
    for step in range(late):
        block = blocks[step // 2][step % 2]
        if step % 2 and len(blocks) > late // 2:
            block = blocks[-1][step // 2]
        held[step] = held_ref[step]
        held[step, :, begin : begin + size] = block.T
        owner = jnp.bitwise_xor(me, first + step)
        window = pl.ds(pl.multiple_of(owner * rows, rows), rows)
        copies += copy_all([pltpu.make_async_copy(held.at[step], out.at[window], sems.at[step])])
    for copy in copies:
        copy.wait()


def on_device(vectors, leaf_basis, transfer, core_mats, row_basis, box_order):
    boxes = transfer.shape[3]
    half = boxes // 2
    rank = leaf_basis.shape[1]
    columns = vectors.shape[1]
    levels = transfer.shape[0]
    inner = lax.axis_size("inner")
    piece = vectors.shape[0] // inner
    width = min(piece, vectors.shape[0] // boxes)
    edges = [columns * sum(PARTS[:n]) // sum(PARTS) for n in range(len(PARTS) + 1)]
    cuts = [(a, b - a) for a, b in zip(edges, edges[1:])]
    count = len(cuts)
    groups = [["abcdefgh".index(x) for x in names] for names in GROUPS]
    spans = [(cuts[m[0]][0], sum(cuts[x][1] for x in m)) for m in groups]
    held = [None] * count
    parted = [None] * count
    done = [[None] * (inner // 2) for _ in groups]
    swaps = [[] for _ in groups]
    early = inner // 4
    level_w = inside = joint = after = None

    for step in ORDER:
        kind, n = step[0], "abcdefgh".find(step[-1])
        g = [names[0] for names in GROUPS].index(step[-1]) if kind in "oquepy" else 0
        if kind == "f":
            firsts = [cuts[0], (cuts[1][0], columns - cuts[1][0])]
            sent_a, kept_a, sent_b, kept_b = call(
                functools.partial(leaf_kernel, firsts),
                [arr(half, size, rank) for _, size in firsts for _ in range(2)],
                [vectors, leaf_basis],
                [HBM] * 2,
                [
                    pltpu.VMEM((2, vectors.shape[0] // 2, columns), jnp.bfloat16),
                    pltpu.VMEM((2, vectors.shape[0] // 2, rank), jnp.bfloat16),
                    pltpu.SemaphoreType.DMA((2, 2)),
                ],
                name="leaves",
                room=LEAF_ROOM,
            )
            got_a, got_b = swapped(sent_a, "inner", 1), swapped(sent_b, "inner", 1)
            held = [(kept_a, got_a, 0)]
            held += [(kept_b, got_b, begin - cuts[1][0]) for begin, _ in cuts[1:]]
            held = list(held)
            after = kept_b
        elif kind == "w":
            level_w = call(
                load_kernel,
                [arr(boxes, 2 * rank, rank)],
                [transfer, after],
                [HBM, ANY],
                [pltpu.SemaphoreType.DMA((2,))],
                name="weights",
                room=LOAD_ROOM,
            )[0]
            after = level_w
        elif kind == "i":
            inside = call(
                inside_kernel,
                [arr(vectors.shape[0] // width, rank, width)],
                [core_mats, row_basis, after],
                [VMEM, VMEM, ANY],
                name="inside",
            )[0]
            after = inside
        elif kind == "j":
            joint, slots = call(
                functools.partial(join_kernel, levels - 1),
                [
                    arr(vectors.shape[0] // width, 2 * rank, width),
                    jax.ShapeDtypeStruct((boxes, 8, 128), jnp.int32),
                ],
                [box_order, transfer, inside, after],
                [SMEM, VMEM, VMEM, ANY],
                name="join",
            )
            after = joint
        elif kind in "msk":
            level = int(step[1])
            size = cuts[n][1]
            sides = {"m": (0, 1), "s": (0,), "k": (1,)}[kind]
            kept, got, begin = parted[n] if kind == "k" else held[n]
            outs = call(
                functools.partial(merge_kernel, level, begin, size, sides),
                [arr(half, size, rank)] * len(sides),
                [kept, got, transfer if level else level_w, after],
                [VMEM, VMEM, VMEM, ANY],
                name={"m": "merge", "s": "sent", "k": "kept"}[kind] + step[1:],
            )
            after = outs[-1]
            if kind == "s":
                parted[n] = held[n]
            if kind != "k":
                axis, bit = level_axis(level + 1)
                arriving = swapped(outs[0], axis, 1 << bit)
            if kind == "m":
                held[n] = (outs[1], arriving, 0)
            elif kind == "s":
                held[n] = (None, arriving, 0)
            else:
                held[n] = (outs[0], held[n][1], 0)
        elif kind in "oe":
            apart = kind == "e"
            which = {"f": "far", "n": "near"}.get(step[1:-1], "last")
            pairs = range(early if which == "far" else 0, early if which == "near" else inner // 2)
            members = groups[g]
            size = spans[g][1]
            states = [x for m in members for x in held[m][:2]]
            outs = call(
                functools.partial(
                    last_kernel,
                    levels - 1,
                    pairs,
                    apart,
                    [(held[m][2], cuts[m][1]) for m in members],
                ),
                [arr(len(pairs), size, piece)] * 2 if apart else [arr(2, size, piece)] * len(pairs),
                [slots, joint, after, *states],
                [VMEM, VMEM, ANY] + [VMEM] * len(states),
                name=which + step[-1],
            )
            after = outs[0]
            if apart:
                coupled = [outs[0], swapped(outs[1], "inner", 1)]
            else:
                for t, x in zip(pairs, outs):
                    done[g][t] = (swapped(x, "inner", 2 * t) if t else x, 0)
        elif kind == "p":
            outs = call(
                couple_kernel,
                [arr(2, spans[g][1], piece)] * (inner // 2 - early),
                coupled + [after],
                [VMEM, VMEM, ANY],
                name=f"couple{step[-1]}",
            )
            after = outs[0]
            for t, x in enumerate(outs, early):
                done[g][t] = (swapped(x, "inner", 2 * t), 0)
        elif kind == "y":
            after = call(
                space_kernel,
                [arr(16, 128)],
                [after] + [x for x, _ in done[g]],
                [ANY] * (1 + len(done[g])),
                name=f"hold{step[-1]}",
            )[0]
        elif kind == "x":
            first = [x for part in swaps[:-2] for x in part]
            after = call(
                space_kernel, [arr(16, 128)], [after, *first], [ANY] * (1 + len(first)), name="space"
            )[0]
        elif kind in "qu":
            pairs = inner // 2
            begin = 0
            end = early if kind == "u" else pairs
            if begin < end:
                turns = list(range(end - begin))
                group = [done[g][begin + t][0] for t in turns]
                bases = [done[g][begin + t][1] for t in turns]
                after = call(
                    functools.partial(pack_kernel, turns, bases),
                    [arr(len(group), spans[g][1], piece)],
                    group + [after],
                    [VMEM] * len(group) + [ANY],
                    name=f"pack{step[-1]}",
                )[0]
                swaps[g].append(swapped(after, "inner", 1))
        elif kind == "z":
            counts = [len(a) + len(b) for a, b in zip(done[:-1], swaps)] + [early + 1]
            turns = list(range(inner // 2))
            flat = [x for d, w in zip(done[:-1], swaps) for x in [d[t][0] for t in turns] + w]
            bases = [[x[1] for x in d] for d in done[:-1]] + [[0] * early]
            flat += [x for x, _ in done[-1][:early]] + swaps[-1][:1]
            placed, rest = call(
                functools.partial(place_kernel, spans, counts, early, turns, bases),
                [arr(*vectors.shape), arr(inner - 2 * early, piece, columns)],
                flat + [after],
                [VMEM] * len(flat) + [ANY],
                [
                    pltpu.VMEM((2 * early, piece, columns), jnp.bfloat16),
                    pltpu.SemaphoreType.DMA((2 * early,)),
                ],
                name="place",
                out_specs=[HBM, VMEM],
            )
            after = rest
    flat = [x for x, _ in done[-1][early:]] + swaps[-1][1:]
    return call(
        functools.partial(finish_kernel, spans[-1]),
        [arr(*vectors.shape)],
        [placed, rest, *flat],
        [HBM, VMEM] + [VMEM] * len(flat),
        [
            pltpu.VMEM((inner - 2 * early, piece, columns), jnp.bfloat16),
            pltpu.SemaphoreType.DMA((inner - 2 * early,)),
        ],
        name="finish",
        out_specs=[HBM],
        aliases={0: 0},
    )[0]


def solution(mesh):
    in_specs = (
        P(("outer", "inner"), None),
        P(("outer", "inner"), None),
        P(None, "outer", "inner", None, None, None),
        P("outer", "inner", None, None, None),
        P(("outer", "inner"), None),
        P("outer", "inner", None),
    )
    out_specs = P(("outer", "inner"), None)
    return jax.shard_map(
        on_device, mesh=mesh, in_specs=in_specs, out_specs=out_specs, check_vma=False
    )
```

```python
import functools

import jax
import jax.numpy as jnp
from jax import lax
from jax.experimental import pallas as pl
from jax.experimental.pallas import tpu as pltpu
from jax.sharding import PartitionSpec as P

INNER_LEVELS = 2
PARTS = (4, 6, 6)
GROUPS = ("a", "b", "c")
COSTS = {
    "lastb": 0.1,
    "lastc": 10,
    "packc": 10,
    "lasta": 2,
    "packa": 10,
    "packb": 10,
    "merge1b": 0.4,
    "join": 0.3,
    "inside": 0.1,
    "merge2a": 0.4,
    "merge1a": 1,
    "place": 10,
    "space": 10,
    "merge1c": 1,
    "weights": 1,
    "merge0a": 10,
    "nearc": 10,
    "farc": 0.4,
    "couplec": 10,
    "holda": 5,
    "sent0a": 5,
    "kept0a": 5,
    "sent1a": 0.5,
    "kept1a": 0.1,
    "sent2c": 1,
    "kept2c": 0.1,
}
ORDER = (
    "f",
    "w",
    "s0a",
    "k0a",
    "m0b",
    "m0c",
    "i",
    "s1a",
    "k1a",
    "m1b",
    "m2a",
    "j",
    "m1c",
    "m2b",
    "oa",
    "s2c",
    "k2c",
    "ob",
    "ya",
    "efc",
    "onc",
    "pc",
    "qa",
    "qb",
    "uc",
    "x",
    "z",
)
LEAF_ROOM = 52
LOAD_ROOM = 48
HBM = pl.BlockSpec(memory_space=pltpu.HBM)
VMEM = pl.BlockSpec(memory_space=pltpu.VMEM)
ANY = pl.BlockSpec(memory_space=pl.ANY)
SMEM = pl.BlockSpec(memory_space=pltpu.SMEM)


def swapped(array, axis, step):
    return lax.ppermute(array, axis, [(i, i ^ step) for i in range(lax.axis_size(axis))])


def level_axis(level):
    return ("inner", level) if level < INNER_LEVELS else ("outer", level - INNER_LEVELS)


def bit_of(level):
    axis, bit = level_axis(level)
    return jnp.bitwise_and(jnp.right_shift(lax.axis_index(axis), bit), 1)


def arr(*shape):
    return jax.ShapeDtypeStruct(shape, jnp.bfloat16)


def dot(a, b, dims=((1,), (0,))):
    return lax.dot_general(a, b, (dims, ((), ())), preferred_element_type=jnp.float32)


def call(kernel, outs, ins, specs, scratch=(), name=None, room=24, out_specs=None, aliases=None):
    run = pl.pallas_call(
        kernel,
        name=name,
        out_shape=outs,
        in_specs=specs,
        out_specs=out_specs or [VMEM] * len(outs),
        input_output_aliases=aliases or {},
        scratch_shapes=list(scratch),
        compiler_params=pltpu.CompilerParams(vmem_limit_bytes=room * 1024 * 1024),
        cost_estimate=pl.CostEstimate(
            flops=int(COSTS.get(name, 2) * 1e9), bytes_accessed=0, transcendentals=0
        ),
    )
    return list(run(*ins))


def copy_all(copies):
    for copy in copies:
        copy.start()
    return copies


def load_kernel(w_hbm, after_ref, w_out, sems):
    parts = sems.shape[0]
    each = w_out.shape[0] // parts
    loads = copy_all(
        [
            pltpu.make_async_copy(
                w_hbm.at[0, 0, 0, pl.ds(n * each, each)],
                w_out.at[pl.ds(n * each, each)],
                sems.at[n],
            )
            for n in range(parts)
        ]
    )
    for load in loads:
        load.wait()


def leaf_kernel(cuts, x_hbm, v_hbm, *refs):
    outs, (x_ref, v_ref, sems) = refs[:-3], refs[-3:]
    half = outs[0].shape[0]
    flag = bit_of(0)
    depth = x_ref.shape[1]
    rows = depth // half
    loads = []
    for late in range(2):
        side = flag if late else 1 - flag
        at = pl.ds(pl.multiple_of(side * depth, depth), depth)
        loads.append(
            copy_all(
                [
                    pltpu.make_async_copy(x_hbm.at[at], x_ref.at[late], sems.at[0, late]),
                    pltpu.make_async_copy(v_hbm.at[at], v_ref.at[late], sems.at[1, late]),
                ]
            )
        )
    for late in range(2):
        for load in loads[late]:
            load.wait()
        for slot in range(half):
            at = pl.ds(slot * rows, rows)
            state = dot(x_ref[late, at, :].T, v_ref[late, at, :]).astype(jnp.bfloat16)
            for n, (begin, size) in enumerate(cuts):
                outs[2 * n + late][slot] = state[begin : begin + size]


def inside_kernel(core_ref, u_ref, after_ref, out):
    width = out.shape[2]
    for n in range(out.shape[0]):
        box = n * width // (u_ref.shape[0] // core_ref.shape[2])
        inside = dot(core_ref[0, 0, box], u_ref[n * width : (n + 1) * width, :], ((1,), (1,)))
        out[n] = inside.astype(jnp.bfloat16)


def join_kernel(level, order_ref, w_ref, inside_ref, after_ref, out, slots_out):
    per_box = inside_ref.shape[0] // w_ref.shape[3]
    for box in range(slots_out.shape[0]):
        slots_out[box] = jnp.full(slots_out.shape[1:], order_ref[0, 0, box] // 2, jnp.int32)
    for n in range(out.shape[0]):
        joint = dot(w_ref[level, 0, 0, order_ref[0, 0, n // per_box]], inside_ref[n])
        out[n] = joint.astype(jnp.bfloat16)


def merged(level, begin, size, kept_ref, got_ref, w_ref, k, box):
    rank = kept_ref.shape[2]
    flag = bit_of(level)
    at = pl.ds(begin, size)
    place = (level, 0, 0, box) if len(w_ref.shape) == 6 else (box,)
    mine = w_ref[(*place, pl.ds(pl.multiple_of(flag * rank, rank), rank), slice(None))]
    other = w_ref[(*place, pl.ds(pl.multiple_of((1 - flag) * rank, rank), rank), slice(None))]
    total = dot(kept_ref[k, at, :], mine) + dot(got_ref[k, at, :], other)
    return total.astype(jnp.bfloat16)


def merge_kernel(level, begin, size, sides, kept_ref, got_ref, w_ref, after_ref, *outs):
    half = kept_ref.shape[0]
    flag = bit_of(level + 1)
    for side, out in zip(sides, outs):
        for slot in range(half):
            box = (flag if side else 1 - flag) * half + slot
            out[slot] = merged(level, begin, size, kept_ref, got_ref, w_ref, box // 2, box)


def last_kernel(level, pairs, apart, parts, slots_ref, joint_ref, after_ref, *refs):
    states, outs = refs[: 2 * len(parts)], refs[2 * len(parts) :]
    half = states[0].shape[0]
    me = lax.axis_index("inner")
    width = joint_ref.shape[2]
    piece = outs[0].shape[2]
    per_box = joint_ref.shape[0] // (2 * half)
    for at, t in enumerate(pairs):
        for odd in range(2):
            if apart:
                out = outs[odd].at[at]
            else:
                out = outs[at].at[odd]
            first = jnp.bitwise_xor(me, 2 * t + odd) * (piece // width)
            for n in range(piece // width):
                k = jnp.max(slots_ref[(first + n) // per_box])
                row = 0
                for i, (begin, size) in enumerate(parts):
                    kept_ref, got_ref = states[2 * i : 2 * i + 2]
                    out[row : row + size, n * width : (n + 1) * width] = merged(
                        level, begin, size, kept_ref, got_ref, joint_ref, k, first + n
                    )
                    row += size


def couple_kernel(mine_ref, got_ref, after_ref, *outs):
    for t, out in enumerate(outs):
        out[0] = mine_ref[t]
        out[1] = got_ref[t]


def pack_kernel(turns, bases, *refs):
    out = refs[-1]
    for at, t in enumerate(turns):
        out[t] = refs[at][bases[at] + 1]


def space_kernel(*refs):
    refs[-1][...] = jnp.zeros_like(refs[-1])


def place_kernel(cuts, counts, early, turns, bases, *refs):
    out, held_out, held, sems = refs[-4:]
    rows = refs[0].shape[2]
    owners = out.shape[0] // rows
    me = lax.axis_index("inner")
    copies = []
    for step in range(owners):
        whole = step < 2 * early
        block_out = held.at[step] if whole else held_out.at[step - 2 * early]
        for n, (begin, size) in enumerate(cuts[: None if whole else -1]):
            at = sum(counts[:n])
            chunk = refs[at : at + counts[n]]
            block = chunk[turns.index(step // 2) if n < len(cuts) - 1 else step // 2][
                bases[n][step // 2]
            ]
            if step % 2:
                mine = early if n == len(cuts) - 1 else owners // 2
                late = [(ref, t) for ref in chunk[mine:] for t in range(ref.shape[0])]
                ref, t = late[step // 2]
                block = ref[t]
            block_out[:, begin : begin + size] = block.T
        if whole:
            owner = jnp.bitwise_xor(me, step)
            window = pl.ds(pl.multiple_of(owner * rows, rows), rows)
            copies += copy_all(
                [pltpu.make_async_copy(held.at[step], out.at[window], sems.at[step])]
            )
    for copy in copies:
        copy.wait()


def finish_kernel(cut, first_ref, held_ref, *refs):
    blocks, (out, held, sems) = refs[:-3], refs[-3:]
    begin, size = cut
    rows = held.shape[1]
    late = held.shape[0]
    first = out.shape[0] // rows - late
    me = lax.axis_index("inner")
    copies = []
    for step in range(late):
        block = blocks[step // 2][step % 2]
        if step % 2 and len(blocks) > late // 2:
            block = blocks[-1][step // 2]
        held[step] = held_ref[step]
        held[step, :, begin : begin + size] = block.T
        owner = jnp.bitwise_xor(me, first + step)
        window = pl.ds(pl.multiple_of(owner * rows, rows), rows)
        copies += copy_all([pltpu.make_async_copy(held.at[step], out.at[window], sems.at[step])])
    for copy in copies:
        copy.wait()


def on_device(vectors, leaf_basis, transfer, core_mats, row_basis, box_order):
    boxes = transfer.shape[3]
    half = boxes // 2
    rank = leaf_basis.shape[1]
    columns = vectors.shape[1]
    levels = transfer.shape[0]
    inner = lax.axis_size("inner")
    piece = vectors.shape[0] // inner
    width = min(piece, vectors.shape[0] // boxes)
    edges = [columns * sum(PARTS[:n]) // sum(PARTS) for n in range(len(PARTS) + 1)]
    cuts = [(a, b - a) for a, b in zip(edges, edges[1:])]
    count = len(cuts)
    groups = [["abcdefgh".index(x) for x in names] for names in GROUPS]
    spans = [(cuts[m[0]][0], sum(cuts[x][1] for x in m)) for m in groups]
    held = [None] * count
    parted = [None] * count
    done = [[None] * (inner // 2) for _ in groups]
    swaps = [[] for _ in groups]
    early = inner // 4
    level_w = inside = joint = after = None

    for step in ORDER:
        kind, n = step[0], "abcdefgh".find(step[-1])
        g = [names[0] for names in GROUPS].index(step[-1]) if kind in "oquepy" else 0
        if kind == "f":
            firsts = [cuts[0], (cuts[1][0], columns - cuts[1][0])]
            sent_a, kept_a, sent_b, kept_b = call(
                functools.partial(leaf_kernel, firsts),
                [arr(half, size, rank) for _, size in firsts for _ in range(2)],
                [vectors, leaf_basis],
                [HBM] * 2,
                [
                    pltpu.VMEM((2, vectors.shape[0] // 2, columns), jnp.bfloat16),
                    pltpu.VMEM((2, vectors.shape[0] // 2, rank), jnp.bfloat16),
                    pltpu.SemaphoreType.DMA((2, 2)),
                ],
                name="leaves",
                room=LEAF_ROOM,
            )
            got_a, got_b = swapped(sent_a, "inner", 1), swapped(sent_b, "inner", 1)
            held = [(kept_a, got_a, 0)]
            held += [(kept_b, got_b, begin - cuts[1][0]) for begin, _ in cuts[1:]]
            held = list(held)
            after = kept_b
        elif kind == "w":
            level_w = call(
                load_kernel,
                [arr(boxes, 2 * rank, rank)],
                [transfer, after],
                [HBM, ANY],
                [pltpu.SemaphoreType.DMA((2,))],
                name="weights",
                room=LOAD_ROOM,
            )[0]
            after = level_w
        elif kind == "i":
            inside = call(
                inside_kernel,
                [arr(vectors.shape[0] // width, rank, width)],
                [core_mats, row_basis, after],
                [VMEM, VMEM, ANY],
                name="inside",
            )[0]
            after = inside
        elif kind == "j":
            joint, slots = call(
                functools.partial(join_kernel, levels - 1),
                [
                    arr(vectors.shape[0] // width, 2 * rank, width),
                    jax.ShapeDtypeStruct((boxes, 8, 128), jnp.int32),
                ],
                [box_order, transfer, inside, after],
                [SMEM, VMEM, VMEM, ANY],
                name="join",
            )
            after = joint
        elif kind in "msk":
            level = int(step[1])
            size = cuts[n][1]
            sides = {"m": (0, 1), "s": (0,), "k": (1,)}[kind]
            kept, got, begin = parted[n] if kind == "k" else held[n]
            outs = call(
                functools.partial(merge_kernel, level, begin, size, sides),
                [arr(half, size, rank)] * len(sides),
                [kept, got, transfer if level else level_w, after],
                [VMEM, VMEM, VMEM, ANY],
                name={"m": "merge", "s": "sent", "k": "kept"}[kind] + step[1:],
            )
            after = outs[-1]
            if kind == "s":
                parted[n] = held[n]
            if kind != "k":
                axis, bit = level_axis(level + 1)
                arriving = swapped(outs[0], axis, 1 << bit)
            if kind == "m":
                held[n] = (outs[1], arriving, 0)
            elif kind == "s":
                held[n] = (None, arriving, 0)
            else:
                held[n] = (outs[0], held[n][1], 0)
        elif kind in "oe":
            apart = kind == "e"
            which = {"f": "far", "n": "near"}.get(step[1:-1], "last")
            pairs = range(early if which == "far" else 0, early if which == "near" else inner // 2)
            members = groups[g]
            size = spans[g][1]
            states = [x for m in members for x in held[m][:2]]
            outs = call(
                functools.partial(
                    last_kernel,
                    levels - 1,
                    pairs,
                    apart,
                    [(held[m][2], cuts[m][1]) for m in members],
                ),
                [arr(len(pairs), size, piece)] * 2 if apart else [arr(2, size, piece)] * len(pairs),
                [slots, joint, after, *states],
                [VMEM, VMEM, ANY] + [VMEM] * len(states),
                name=which + step[-1],
            )
            after = outs[0]
            if apart:
                coupled = [outs[0], swapped(outs[1], "inner", 1)]
            else:
                for t, x in zip(pairs, outs):
                    done[g][t] = (swapped(x, "inner", 2 * t) if t else x, 0)
        elif kind == "p":
            outs = call(
                couple_kernel,
                [arr(2, spans[g][1], piece)] * (inner // 2 - early),
                coupled + [after],
                [VMEM, VMEM, ANY],
                name=f"couple{step[-1]}",
            )
            after = outs[0]
            for t, x in enumerate(outs, early):
                done[g][t] = (swapped(x, "inner", 2 * t), 0)
        elif kind == "y":
            after = call(
                space_kernel,
                [arr(16, 128)],
                [after] + [x for x, _ in done[g]],
                [ANY] * (1 + len(done[g])),
                name=f"hold{step[-1]}",
            )[0]
        elif kind == "x":
            first = [x for part in swaps[:-2] for x in part]
            after = call(
                space_kernel, [arr(16, 128)], [after, *first], [ANY] * (1 + len(first)), name="space"
            )[0]
        elif kind in "qu":
            pairs = inner // 2
            begin = 0
            end = early if kind == "u" else pairs
            if begin < end:
                turns = list(range(end - begin))
                group = [done[g][begin + t][0] for t in turns]
                bases = [done[g][begin + t][1] for t in turns]
                after = call(
                    functools.partial(pack_kernel, turns, bases),
                    [arr(len(group), spans[g][1], piece)],
                    group + [after],
                    [VMEM] * len(group) + [ANY],
                    name=f"pack{step[-1]}",
                )[0]
                swaps[g].append(swapped(after, "inner", 1))
        elif kind == "z":
            counts = [len(a) + len(b) for a, b in zip(done[:-1], swaps)] + [early + 1]
            turns = list(range(inner // 2))
            flat = [x for d, w in zip(done[:-1], swaps) for x in [d[t][0] for t in turns] + w]
            bases = [[x[1] for x in d] for d in done[:-1]] + [[0] * early]
            flat += [x for x, _ in done[-1][:early]] + swaps[-1][:1]
            placed, rest = call(
                functools.partial(place_kernel, spans, counts, early, turns, bases),
                [arr(*vectors.shape), arr(inner - 2 * early, piece, columns)],
                flat + [after],
                [VMEM] * len(flat) + [ANY],
                [
                    pltpu.VMEM((2 * early, piece, columns), jnp.bfloat16),
                    pltpu.SemaphoreType.DMA((2 * early,)),
                ],
                name="place",
                out_specs=[HBM, VMEM],
            )
            after = rest
    flat = [x for x, _ in done[-1][early:]] + swaps[-1][1:]
    return call(
        functools.partial(finish_kernel, spans[-1]),
        [arr(*vectors.shape)],
        [placed, rest, *flat],
        [HBM, VMEM] + [VMEM] * len(flat),
        [
            pltpu.VMEM((inner - 2 * early, piece, columns), jnp.bfloat16),
            pltpu.SemaphoreType.DMA((inner - 2 * early,)),
        ],
        name="finish",
        out_specs=[HBM],
        aliases={0: 0},
    )[0]


def solution(mesh):
    in_specs = (
        P(("outer", "inner"), None),
        P(("outer", "inner"), None),
        P(None, "outer", "inner", None, None, None),
        P("outer", "inner", None, None, None),
        P(("outer", "inner"), None),
        P("outer", "inner", None),
    )
    out_specs = P(("outer", "inner"), None)
    return jax.shard_map(
        on_device, mesh=mesh, in_specs=in_specs, out_specs=out_specs, check_vma=False
    )
```
